128 devices in a mesh: tm: 32 (over y, x, core), hid: 4 (over z).
Axes of the slice: x: 4, y: 4, z: 4, core: 2. Of those that a mesh axis runs over, the one named last changes fastest.
Arguments:
- gate_inputs: bfloat16 [8192, 3, 4096], P('tm', None, 'hid'), may hold values from -6 to 16
- recurrent: bfloat16 [3, 4096, 4096], P(None, None, 'hid'), may hold values from -0.09375 to 0.09375
- initial_state: float32 [4096], P('hid'), may hold values from -0.9 to 0.9
- guess: bfloat16 [8192, 4096], P('tm', 'hid'), may hold values from -0.8984375 to 0.8984375
Outputs:
- trajectory: bfloat16 [8192, 4096], P('tm', 'hid')
The draws below stay inside these ranges and needn't reach their ends.
All inputs are finite; a program needn't handle non-finite values.
Results may differ from the reference program's by a relative error of at most 0.003.
Values may be sent and summed in bfloat16 or wider, within the bound.
A program may use at most 128 MiB of HBM per device.

```python
import math
import jax
import jax.numpy as jnp
from jax import lax

HIDDEN_UNITS = 4096
ITERS = 2
TIME_STEPS = 8192


def draw_gate_inputs(key, part):
    random_keys = jax.random.split(key, 6)
    slow_share = 0.5
    random_noise = jnp.clip(jax.random.normal(random_keys[0], (TIME_STEPS, 3, HIDDEN_UNITS), jnp.float32), -4.0, 4.0)
    chosen = jax.random.uniform(random_keys[1], (HIDDEN_UNITS,), jnp.float32) < slow_share
    slow_rate = jax.random.uniform(random_keys[2], (HIDDEN_UNITS,), jnp.float32, 0.2, 1.0) * 2.0 / TIME_STEPS
    fast_rate = jnp.exp(jax.random.uniform(random_keys[3], (HIDDEN_UNITS,), jnp.float32, math.log(1.0 / 50.0), math.log(1.0 / 3.0)))
    decay_rate = jnp.where(chosen, slow_rate, fast_rate)
    constant_input = jnp.log((1.0 - decay_rate) / decay_rate)
    spike_rows = jax.random.randint(random_keys[4], (4,), 0, TIME_STEPS)
    spike_input = jnp.any(jnp.arange(TIME_STEPS)[:, None] == spike_rows[None, :], axis=1)
    spike_logit = jax.random.uniform(random_keys[5], (TIME_STEPS, HIDDEN_UNITS), jnp.float32, 0.0, 1.4)
    update_portion = jnp.where(spike_input[:, None], spike_logit, constant_input[None, :]) + 0.3 * random_noise[:, 0]
    reset_part = random_noise[:, 1]
    candidate_part = 1.5 * random_noise[:, 2]
    stacked = jnp.stack([update_portion, reset_part, candidate_part], axis=1)
    return stacked.astype(jnp.bfloat16)


def levels(own_key, extent, cuts, smallest, high):
    def one(position, shards_of):
        draws = jax.random.uniform(jax.random.fold_in(jax.random.fold_in(own_key, 6), position), (shards_of,), jnp.float32, smallest / len(cuts), high / len(cuts))
        return jnp.repeat(jnp.exp(draws), extent[position] // shards_of).reshape((-1,) + (1,) * (len(extent) - position - 1))

    level = one(*cuts[0])
    for cut in cuts[1:]:
        level = level * one(*cut)
    return level


def gaussian(key, shape, deviation, bound, cuts=(), dtype=jnp.bfloat16):
    drawn = jax.random.normal(key, shape, jnp.float32) * deviation
    if len(cuts) > 0:
        drawn = levels(key, shape, cuts, -0.22, 0.18) * drawn
    return jnp.clip(drawn, min=-bound, max=bound).astype(dtype)


def setup_inputs(seed: int = 0) -> dict:
    streams_of = jax.random.split(jax.random.key(seed), 5)
    return {
        "gate_inputs": draw_gate_inputs(jax.random.fold_in(streams_of[4], 71), 0),
        "recurrent": gaussian(streams_of[1], (3, HIDDEN_UNITS, HIDDEN_UNITS), HIDDEN_UNITS ** -0.5, 0.09375, ((2, 4),)),
        "initial_state": jnp.clip(jax.random.uniform(streams_of[2], (HIDDEN_UNITS,), jnp.float32, -0.9, 0.9) * levels(streams_of[2], (HIDDEN_UNITS,), ((0, 4),), -0.4, 0.0), -0.9, 0.9),
        "guess": jnp.clip(jax.random.uniform(streams_of[3], (TIME_STEPS, HIDDEN_UNITS), jnp.float32, -0.8984375, 0.8984375) * levels(streams_of[3], (TIME_STEPS, HIDDEN_UNITS), ((0, 32), (1, 4)), -0.4, 0.0), -0.8984375, 0.8984375).astype(jnp.bfloat16),
    }


def compose(earlier, later):
    earlier_gain, earlier_shift = earlier
    later_gain, later_shift = later
    return later_gain * earlier_gain, later_gain * earlier_shift + later_shift


def cell_terms(inputs, previous, recurrent, diagonal):
    rounded = previous.astype(jnp.bfloat16)
    update_pre = jnp.dot(rounded, recurrent[0], preferred_element_type=jnp.float32)
    reset_pre = jnp.dot(rounded, recurrent[1], preferred_element_type=jnp.float32)
    memory = jnp.dot(rounded, recurrent[2], preferred_element_type=jnp.float32)
    update = jax.nn.sigmoid(inputs[:, 0] + update_pre)
    reset = jax.nn.sigmoid(inputs[:, 1] + reset_pre)
    candidate = jnp.tanh(inputs[:, 2] + reset * memory)
    target = (1.0 - update) * candidate + update * previous
    slope = (update * (1.0 - update) * diagonal[0] * (previous - candidate)
             + (1.0 - update) * (1.0 - candidate * candidate)
             * (reset * (1.0 - reset) * diagonal[1] * memory + reset * diagonal[2])
             + update)
    return slope, target - slope * previous


def reference(gate_inputs, recurrent, initial_state, guess):
    inputs = gate_inputs.astype(jnp.float32)
    diagonal = jnp.diagonal(recurrent, axis1=1, axis2=2).astype(jnp.float32)
    states = guess.astype(jnp.float32)
    for step in range(ITERS):
        previous = jnp.concatenate([initial_state[None, :], states[:-1]], axis=0)
        slope, offset = cell_terms(inputs, previous, recurrent, diagonal)
        gains, shifts = lax.associative_scan(compose, (slope, offset), axis=0)
        states = gains * initial_state[None, :] + shifts
    return states.astype(jnp.bfloat16)
```

```python
import functools

import jax
import jax.numpy as jnp
from jax import lax
from jax.experimental import pallas as pl
from jax.experimental.pallas import tpu as pltpu
from jax.sharding import PartitionSpec as P

ITERS = 2
ROWS = 256
UNITS = 1024
SUB = 16
CW = 256
NC = UNITS // CW
GROUP = 8
LINES = 4
MESH = pl.DeviceIdType.MESH


def dot(a, b):
    return jnp.dot(a, b, preferred_element_type=jnp.float32)


def sigmoid(x):
    return 0.5 * jnp.tanh(0.5 * x) + 0.5


def kernel(
    gi, w, h0, guess, out,
    wv, giv, gv, xb, acc, ip, hprev, gs, ss, eg, es, diag, bnd, tot1, tot2, got1, got2, perm, states, outv,
    load_sem, w_sem, out_sem, bnd_sem, right_s, left_s, fwd_s, z_r, edge_s, edge_r, s1, r1, s2, r2,
):
    tm = lax.axis_index("tm")
    z = lax.axis_index("hid")
    y, q = tm // GROUP, lax.rem(tm, GROUP)
    right, left = lax.rem(z + 1, 4), lax.rem(z + 3, 4)

    load_guess = pltpu.make_async_copy(guess, gv, load_sem.at[0])
    load_inputs = pltpu.make_async_copy(gi, giv, load_sem.at[1])

    def load_weights(d):
        rows = pl.ds(pl.multiple_of(lax.rem(z + d, 4) * UNITS, UNITS), UNITS)
        return pltpu.make_async_copy(w.at[:, rows, :], wv.at[d], w_sem.at[d])

    load_guess.start()
    load_weights(0).start()
    load_inputs.start()
    for d in (1, 3, 2):
        load_weights(d).start()

    barrier = pltpu.get_barrier_semaphore()

    def greet(device):
        pl.semaphore_signal(barrier, inc=1, device_id=device, device_id_type=MESH)

    greet((tm, right))
    greet((tm, left))
    greet((lax.rem(tm + 1, 32), z))
    greet((lax.rem(tm + 31, 32), z))
    for j in range(1, GROUP):
        greet((y * GROUP + lax.rem(q + j, GROUP), z))
    for j in range(1, LINES):
        greet((lax.rem(y + j, LINES) * GROUP + q, z))

    r = lax.broadcasted_iota(jnp.int32, (ROWS, ROWS), 0)
    t = lax.broadcasted_iota(jnp.int32, (ROWS, ROWS), 1)
    time = (r & (SUB - 1)) * SUB + (r >> 4)
    perm[0] = jnp.where(t == time, 1.0, 0.0).astype(jnp.bfloat16)
    perm[1] = jnp.where(t == time - 1, 1.0, 0.0).astype(jnp.bfloat16)

    load_guess.wait()

    def shift(n, carry):
        cols = pl.ds(pl.multiple_of(n * CW, CW), CW)
        rows = dot(perm[1], gv[:, cols])
        hprev[n] = rows
        xb[0, 0, n] = rows.astype(jnp.bfloat16)
        return carry

    lax.fori_loop(0, NC, shift, 0)

    pl.semaphore_wait(barrier, 4 + (GROUP - 1) + (LINES - 1))

    def remote(src, dst, send, recv, device):
        return pltpu.make_async_remote_copy(
            src_ref=src, dst_ref=dst, send_sem=send, recv_sem=recv, device_id=device, device_id_type=MESH
        )

    def part(it, d, c):
        return xb.at[it, d, c, pl.ds(SUB, ROWS - SUB), :] if it == 0 else xb.at[it, d, c]

    def to_right(it, c):
        return remote(part(it, 0, c), part(it, 3, c), right_s.at[it, c], z_r.at[it, 3, c], (tm, right))

    def to_left(it, c):
        return remote(part(it, 0, c), part(it, 1, c), left_s.at[it, c], z_r.at[it, 1, c], (tm, left))

    def forward(it, c):
        src, device = (3, right) if c < NC // 2 else (1, left)
        return remote(part(it, src, c), part(it, 2, c), fwd_s.at[it, c], z_r.at[it, 2, c], (tm, device))

    def edge(d, lo, hi):
        return xb.at[0, d, pl.ds(lo, hi - lo), pl.ds(0, SUB), :]

    half = NC // 2
    edges = (
        remote(edge(0, 0, NC), edge(3, 0, NC), edge_s.at[0], edge_r.at[0], (tm, right)),
        remote(edge(0, 0, NC), edge(1, 0, NC), edge_s.at[1], edge_r.at[1], (tm, left)),
        remote(edge(3, 0, half), edge(2, 0, half), edge_s.at[2], edge_r.at[2], (tm, right)),
        remote(edge(1, half, NC), edge(2, half, NC), edge_s.at[3], edge_r.at[3], (tm, left)),
    )

    boundary = remote(
        guess.at[pl.ds(ROWS - SUB, SUB), :], bnd, bnd_sem.at[0], bnd_sem.at[1], (lax.rem(tm + 1, 32), z)
    )
    boundary.start()
    for c in range(half):
        to_right(0, c).start()
        to_left(0, half + c).start()
    boundary.wait_recv()
    first = lax.broadcasted_iota(jnp.int32, (SUB, CW), 0) == 0
    for n in range(NC):
        cols = slice(n * CW, (n + 1) * CW)
        row = jnp.where(tm == 0, h0[:, cols], bnd[SUB - 1 :, cols].astype(jnp.float32))
        tile = jnp.where(first, row, hprev[n, 0:SUB, :])
        hprev[n, 0:SUB, :] = tile
        xb[0, 0, n, 0:SUB, :] = tile.astype(jnp.bfloat16)
    edges[0].start()
    edges[1].start()
    for c in range(half):
        to_right(0, half + c).start()
        to_left(0, c).start()

    load_inputs.wait()

    def order_inputs(n, carry):
        cols = pl.ds(pl.multiple_of(n * CW, CW), CW)
        for g in range(3):
            ip[n, g] = dot(perm[0], giv[g, :, cols])
        return carry

    lax.fori_loop(0, NC, order_inputs, 0)

    def accumulate(it, pairs, start):
        def body(n, carry):
            cols = pl.ds(pl.multiple_of(n * CW, CW), CW)
            for g in range(3):
                total = None
                for d, c in pairs:
                    term = dot(xb[it, d, c], wv[d, g, c * CW : (c + 1) * CW, cols])
                    total = term if total is None else total + term
                acc[n, g] = total if start else acc[n, g] + total
            return carry

        lax.fori_loop(0, NC, body, 0)

    sub_row = lax.broadcasted_iota(jnp.int32, (SUB, CW), 0)

    def tile_of(i):
        return slice(i * SUB, (i + 1) * SUB)

    def stage1(it, n, j):
        device = (y * GROUP + lax.rem(q + j, GROUP), z)
        return remote(tot1.at[it, n], got1.at[it, n, q], s1.at[it, n, j], r1.at[it, n, q], device)

    def stage2(it, n, j):
        device = (lax.rem(y + j, LINES) * GROUP + q, z)
        return remote(tot2.at[it, n], got2.at[it, n, y], s2.at[it, n, j], r2.at[it, n, y], device)

    def gates(it, n):
        d0, d1, d2 = (jnp.broadcast_to(diag[n, g : g + 1, :], (SUB, CW)) for g in range(3))
        gain = shift_ = None
        for i in range(ROWS // SUB):
            rows = tile_of(i)
            previous = hprev[n, rows, :]
            memory = acc[n, 2, rows, :]
            update = sigmoid(ip[n, 0, rows, :] + acc[n, 0, rows, :])
            reset = sigmoid(ip[n, 1, rows, :] + acc[n, 1, rows, :])
            candidate = jnp.tanh(ip[n, 2, rows, :] + reset * memory)
            keep = 1.0 - update
            gap = previous - candidate
            target = candidate + update * gap
            slope = update + keep * (
                update * gap * d0
                + (1.0 - candidate * candidate) * reset * ((1.0 - reset) * memory * d1 + d2)
            )
            offset = target - slope * previous
            gain = slope if gain is None else slope * gain
            shift_ = offset if shift_ is None else slope * shift_ + offset
            gs[n, rows, :] = gain
            ss[n, rows, :] = shift_
        for k in (1, 2, 4, 8):
            before_gain = jnp.where(sub_row < k, 1.0, pltpu.roll(gain, k, 0))
            before_shift = jnp.where(sub_row < k, 0.0, pltpu.roll(shift_, k, 0))
            shift_ = gain * before_shift + shift_
            gain = gain * before_gain
        eg[n] = jnp.where(sub_row < 1, 1.0, pltpu.roll(gain, 1, 0))
        es[n] = jnp.where(sub_row < 1, 0.0, pltpu.roll(shift_, 1, 0))
        tot1[it, n, 0:1, :] = gain[SUB - 1 :, :]
        tot1[it, n, 1:2, :] = shift_[SUB - 1 :, :]
        got1[it, n, q, 0:1, :] = gain[SUB - 1 :, :]
        got1[it, n, q, 1:2, :] = shift_[SUB - 1 :, :]

        def send(j, carry):
            stage1(it, n, j).start()
            return carry

        lax.fori_loop(1, GROUP, send, 0)

    def middle(it, n):
        def receive(j, carry):
            source = lax.rem(q + j, GROUP)
            remote(tot1.at[it, n], got1.at[it, n, source], s1.at[it, n, j], r1.at[it, n, source], (tm, z)).wait_recv()
            return carry

        lax.fori_loop(1, GROUP, receive, 0)
        all_gain = jnp.ones((1, CW), jnp.float32)
        all_shift = jnp.zeros((1, CW), jnp.float32)
        my_gain, my_shift = all_gain, all_shift
        for p in range(GROUP):
            g, s = got1[it, n, p, 0:1, :], got1[it, n, p, 1:2, :]
            all_shift = g * all_shift + s
            all_gain = g * all_gain
            my_gain = jnp.where(p < q, all_gain, my_gain)
            my_shift = jnp.where(p < q, all_shift, my_shift)
        tot1_n = n
        tot2[it, n, 0:1, :] = all_gain
        tot2[it, n, 1:2, :] = all_shift
        got2[it, n, y, 0:1, :] = all_gain
        got2[it, n, y, 1:2, :] = all_shift
        bnd_gain_shift[n, 0:1, :] = my_gain
        bnd_gain_shift[n, 1:2, :] = my_shift

        def send(j, carry):
            stage2(it, n, j).start()
            return carry

        lax.fori_loop(1, LINES, send, 0)

    bnd_gain_shift = diag.at[:, 3:5, :]

    def entering_state(it, n):
        def receive(j, carry):
            source = lax.rem(y + j, LINES)
            remote(tot2.at[it, n], got2.at[it, n, source], s2.at[it, n, j], r2.at[it, n, source], (tm, z)).wait_recv()
            return carry

        lax.fori_loop(1, LINES, receive, 0)
        state = h0[:, pl.ds(pl.multiple_of(n * CW, CW), CW)]
        for p in range(LINES - 1):
            g, s = got2[it, n, p, 0:1, :], got2[it, n, p, 1:2, :]
            state = jnp.where(p < y, g * state + s, state)
        state = diag[n, 3:4, :] * state + diag[n, 4:5, :]
        return eg[n] * state + es[n]

    def loop(body):
        def step(n, carry):
            body(n)
            return carry

        lax.fori_loop(0, NC, step, 0)

    def apply_middle(n):
        enter = entering_state(0, n)
        hprev[n, 0:SUB, :] = enter
        xb[1, 0, n, 0:SUB, :] = enter.astype(jnp.bfloat16)
        for i in range(ROWS // SUB - 1):
            state = gs[n, tile_of(i), :] * enter + ss[n, tile_of(i), :]
            hprev[n, tile_of(i + 1), :] = state
            xb[1, 0, n, tile_of(i + 1), :] = state.astype(jnp.bfloat16)
        to_right(1, n).start()
        to_left(1, n).start()

    def store_out(n):
        cols = pl.ds(pl.multiple_of(n * CW, CW), CW)
        return pltpu.make_async_copy(outv.at[n], out.at[:, cols], out_sem.at[n])

    def apply_last(n):
        enter = entering_state(1, n)
        for i in range(ROWS // SUB):
            state = gs[n, tile_of(i), :] * enter + ss[n, tile_of(i), :]
            states[n, tile_of(i), :] = state.astype(jnp.bfloat16)
        outv[n] = dot(perm[0], states[n]).astype(jnp.bfloat16)
        store_out(n).start()

    for it in range(ITERS):
        if it == 0:
            load_weights(0).wait()
            same = r == t
            for n in range(NC):
                block = slice(n * CW, (n + 1) * CW)
                for g in range(3):
                    square = wv[0, g, block, block].astype(jnp.float32)
                    diag[n, g : g + 1, :] = jnp.sum(jnp.where(same, square, 0.0), axis=0, keepdims=True)
        accumulate(it, [(0, c) for c in range(NC)], True)
        for c in range(NC):
            if it == 0 and c == 0:
                load_weights(1).wait()
                load_weights(3).wait()
                edges[0].wait_recv()
                edges[2].start()
                edges[1].wait_recv()
                edges[3].start()
            left_c = (c + half) % NC
            to_right(it, c).wait_recv()
            to_left(it, left_c).wait_recv()
            if c < half:
                forward(it, c).start()
                forward(it, left_c).start()
            accumulate(it, [(3, c), (1, left_c)], False)
        if it == 0:
            load_weights(2).wait()
            edges[2].wait_recv()
            edges[3].wait_recv()
        for c in range(half):
            forward(it, c).wait_recv()
            forward(it, c + half).wait_recv()
            accumulate(it, [(2, c), (2, c + half)], False)
        loop(functools.partial(gates, it))
        loop(functools.partial(middle, it))
        loop(apply_middle if it == 0 else apply_last)

    boundary.wait_send()
    for copy in edges:
        copy.wait_send()
    for it in range(ITERS):
        for c in range(NC):
            to_right(it, c).wait_send()
            to_left(it, c).wait_send()
            forward(it, c).wait_send()

        def drain(n):
            def one(j, carry):
                stage1(it, n, j).wait_send()
                return carry

            def two(j, carry):
                stage2(it, n, j).wait_send()
                return carry

            lax.fori_loop(1, GROUP, one, 0)
            lax.fori_loop(1, LINES, two, 0)

        loop(drain)
    loop(lambda n: store_out(n).wait())


def per_device(gate_inputs, recurrent, initial_state, guess):
    bf16, f32 = jnp.bfloat16, jnp.float32
    dma = pltpu.SemaphoreType.DMA
    hbm = pl.BlockSpec(memory_space=pl.ANY)
    vmem = pl.BlockSpec(memory_space=pltpu.VMEM)
    return pl.pallas_call(
        kernel,
        out_shape=jax.ShapeDtypeStruct((ROWS, UNITS), bf16),
        in_specs=[hbm, hbm, vmem, hbm],
        out_specs=hbm,
        scratch_shapes=[
            pltpu.VMEM((4, 3, UNITS, UNITS), bf16),
            pltpu.VMEM((3, ROWS, UNITS), bf16),
            pltpu.VMEM((ROWS, UNITS), bf16),
            pltpu.VMEM((ITERS, 4, NC, ROWS, CW), bf16),
            pltpu.VMEM((NC, 3, ROWS, CW), f32),
            pltpu.VMEM((NC, 3, ROWS, CW), f32),
            pltpu.VMEM((NC, ROWS, CW), f32),
            pltpu.VMEM((NC, ROWS, CW), f32),
            pltpu.VMEM((NC, ROWS, CW), f32),
            pltpu.VMEM((NC, SUB, CW), f32),
            pltpu.VMEM((NC, SUB, CW), f32),
            pltpu.VMEM((NC, 8, CW), f32),
            pltpu.VMEM((SUB, UNITS), bf16),
            pltpu.VMEM((ITERS, NC, 2, CW), f32),
            pltpu.VMEM((ITERS, NC, 2, CW), f32),
            pltpu.VMEM((ITERS, NC, GROUP, 2, CW), f32),
            pltpu.VMEM((ITERS, NC, LINES, 2, CW), f32),
            pltpu.VMEM((2, ROWS, ROWS), bf16),
            pltpu.VMEM((NC, ROWS, CW), bf16),
            pltpu.VMEM((NC, ROWS, CW), bf16),
            dma((2,)),
            dma((4,)),
            dma((NC,)),
            dma((2,)),
            dma((ITERS, NC)),
            dma((ITERS, NC)),
            dma((ITERS, NC)),
            dma((ITERS, 4, NC)),
            dma((4,)),
            dma((4,)),
            dma((ITERS, NC, GROUP)),
            dma((ITERS, NC, GROUP)),
            dma((ITERS, NC, LINES)),
            dma((ITERS, NC, LINES)),
        ],
        compiler_params=pltpu.CompilerParams(
            collective_id=0, has_side_effects=True, vmem_limit_bytes=58 * 2**20
        ),
    )(jnp.transpose(gate_inputs, (1, 0, 2)), recurrent, initial_state[None, :], guess)


def solution(mesh):
    in_specs = (P("tm", None, "hid"), P(None, None, "hid"), P("hid"), P("tm", "hid"))
    return jax.shard_map(
        per_device, mesh=mesh, in_specs=in_specs, out_specs=P("tm", "hid"), check_vma=False
    )
```

```python
import functools

import jax
import jax.numpy as jnp
from jax import lax
from jax.experimental import pallas as pl
from jax.experimental.pallas import tpu as pltpu
from jax.sharding import PartitionSpec as P

ITERS = 2
ROWS = 256
UNITS = 1024
SUB = 16
CW = 256
NC = UNITS // CW
GROUP = 8
LINES = 4
EARLY = 2
XS = 4
STEPS = GROUP * LINES
AWAY = sorted(
    [(a, b, c) for a in range(LINES) for b in range(XS) for c in range(2) if (a, b, c) != (0, 0, 0)],
    key=lambda k: -(min(k[0], LINES - k[0]) + min(k[1], XS - k[1])),
)
MESH = pl.DeviceIdType.MESH


def dot(a, b):
    return jnp.dot(a, b, preferred_element_type=jnp.float32)


def sigmoid(x):
    return 0.5 * jnp.tanh(0.5 * x) + 0.5


def kernel(
    gi, w, h0, guess, out,
    wv, giv, gv, xb, acc, ip, hprev, gs, ss, eg, es, diag, bnd, total, totals, mine, perm, states, outv,
    load_sem, w_sem, out_sem, bnd_sem, right_s, left_s, fwd_s, z_r, edge_s, edge_r, t_s, t_r, known,
):
    tm = lax.axis_index("tm")
    z = lax.axis_index("hid")
    y, q = tm // GROUP, lax.rem(tm, GROUP)
    right, left = lax.rem(z + 1, 4), lax.rem(z + 3, 4)

    load_guess = pltpu.make_async_copy(guess, gv, load_sem.at[0])
    load_inputs = pltpu.make_async_copy(gi, giv, load_sem.at[1])

    def load_weights(d):
        rows = pl.ds(pl.multiple_of(lax.rem(z + d, 4) * UNITS, UNITS), UNITS)
        return pltpu.make_async_copy(w.at[:, rows, :], wv.at[d], w_sem.at[d])

    load_guess.start()
    load_weights(0).start()
    load_inputs.start()
    for d in (1, 3, 2):
        load_weights(d).start()

    barrier = pltpu.get_barrier_semaphore()

    def greet(device):
        pl.semaphore_signal(barrier, inc=1, device_id=device, device_id_type=MESH)

    x, core = q // 2, lax.rem(q, 2)

    def device_at(a, b, c):
        return lax.rem(y + a, LINES) * GROUP + lax.rem(x + b, XS) * 2 + lax.rem(core + c, 2)

    x_pair = ((device_at(0, 1, 0), z), (device_at(0, XS - 1, 0), z))
    y_pair = ((device_at(1, 0, 0), z), (device_at(LINES - 1, 0, 0), z))
    partner = ((device_at(0, 0, 1), z),)
    later = (lax.rem(tm + 1, STEPS), z)
    earlier = (lax.rem(tm + STEPS - 1, STEPS), z)
    near = ((tm, right), (tm, left), later, earlier) + x_pair + y_pair + partner
    for device in near:
        greet(device)

    r = lax.broadcasted_iota(jnp.int32, (ROWS, ROWS), 0)
    t = lax.broadcasted_iota(jnp.int32, (ROWS, ROWS), 1)
    time = (r & (SUB - 1)) * SUB + (r >> 4)
    perm[0] = jnp.where(t == time, 1.0, 0.0).astype(jnp.bfloat16)
    perm[1] = jnp.where(t == time - 1, 1.0, 0.0).astype(jnp.bfloat16)

    load_guess.wait()

    def shift(n, carry):
        cols = pl.ds(pl.multiple_of(n * CW, CW), CW)
        rows = dot(perm[1], gv[:, cols])
        hprev[n] = rows
        xb[0, 0, n] = rows.astype(jnp.bfloat16)
        return carry

    lax.fori_loop(0, NC, shift, 0)

    pl.semaphore_wait(barrier, len(near))

    def remote(src, dst, send, recv, device):
        return pltpu.make_async_remote_copy(
            src_ref=src, dst_ref=dst, send_sem=send, recv_sem=recv, device_id=device, device_id_type=MESH
        )

    def part(it, d, c):
        return xb.at[it, d, c, pl.ds(SUB, ROWS - SUB), :] if it == 0 else xb.at[it, d, c]

    def to_right(it, c):
        return remote(part(it, 0, c), part(it, 3, c), right_s.at[it, c], z_r.at[it, 3, c], (tm, right))

    def to_left(it, c):
        return remote(part(it, 0, c), part(it, 1, c), left_s.at[it, c], z_r.at[it, 1, c], (tm, left))

    def forward(it, c):
        src, device = (3, right) if c < NC // 2 else (1, left)
        return remote(part(it, src, c), part(it, 2, c), fwd_s.at[it, c], z_r.at[it, 2, c], (tm, device))

    def edge(d, lo, hi):
        return xb.at[0, d, pl.ds(lo, hi - lo), pl.ds(0, SUB), :]

    half = NC // 2
    edges = (
        remote(edge(0, 0, NC), edge(3, 0, NC), edge_s.at[0], edge_r.at[0], (tm, right)),
        remote(edge(0, 0, NC), edge(1, 0, NC), edge_s.at[1], edge_r.at[1], (tm, left)),
        remote(edge(3, 0, half), edge(2, 0, half), edge_s.at[2], edge_r.at[2], (tm, right)),
        remote(edge(1, half, NC), edge(2, half, NC), edge_s.at[3], edge_r.at[3], (tm, left)),
    )

    boundary = remote(
        gv.at[pl.ds(ROWS - SUB, SUB), :], bnd, bnd_sem.at[0], bnd_sem.at[1], later
    )
    boundary.start()
    for c in range(EARLY):
        to_right(0, c).start()
        to_left(0, (half + c) % NC).start()

    def tell(k, devices):
        for device in devices:
            pl.semaphore_signal(known.at[k], inc=1, device_id=device, device_id_type=MESH)

    def hear(k, devices):
        pl.semaphore_wait(known.at[k], len(devices))

    tell(0, x_pair)
    boundary.wait_recv()
    first = lax.broadcasted_iota(jnp.int32, (SUB, CW), 0) == 0
    for n in range(NC):
        cols = slice(n * CW, (n + 1) * CW)
        row = jnp.where(tm == 0, h0[:, cols], bnd[SUB - 1 :, cols].astype(jnp.float32))
        tile = jnp.where(first, row, hprev[n, 0:SUB, :])
        hprev[n, 0:SUB, :] = tile
        xb[0, 0, n, 0:SUB, :] = tile.astype(jnp.bfloat16)
    edges[0].start()
    edges[1].start()
    for c in range(EARLY, NC):
        to_right(0, c).start()
        to_left(0, (half + c) % NC).start()
    hear(0, x_pair)
    tell(1, partner)

    load_inputs.wait()

    for n in range(NC):
        for g in range(3):
            ip[n, g] = dot(perm[0], giv[g, :, n * CW : (n + 1) * CW])

    def accumulate(it, pairs, start=False, parts=range(NC)):
        for n in parts:
            cols = slice(n * CW, (n + 1) * CW)
            for g in range(3):
                terms = None if start else acc[n, g]
                for d, c in pairs:
                    term = dot(xb[it, d, c], wv[d, g, c * CW : (c + 1) * CW, cols])
                    terms = term if terms is None else terms + term
                acc[n, g] = terms

    sub_row = lax.broadcasted_iota(jnp.int32, (SUB, CW), 0)

    def tile_of(i):
        return slice(i * SUB, (i + 1) * SUB)

    def total_to(it, away):
        device = device_at(*away)
        copy = remote(total.at[it], totals.at[it, tm], t_s.at[it, device], t_r.at[it, tm], (device, z))
        return device, copy

    def total_from(it, p):
        return remote(total.at[it], totals.at[it, p], t_s.at[it, p], t_r.at[it, p], (tm, right))

    def gates(it, n):
        d0, d1, d2 = (jnp.broadcast_to(diag[n, g : g + 1, :], (SUB, CW)) for g in range(3))
        gain = shift_ = None
        for i in range(ROWS // SUB):
            rows = tile_of(i)
            previous = hprev[n, rows, :]
            memory = acc[n, 2, rows, :]
            update = sigmoid(ip[n, 0, rows, :] + acc[n, 0, rows, :])
            reset = sigmoid(ip[n, 1, rows, :] + acc[n, 1, rows, :])
            candidate = jnp.tanh(ip[n, 2, rows, :] + reset * memory)
            keep = 1.0 - update
            gap = previous - candidate
            target = candidate + update * gap
            slope = update + keep * (
                update * gap * d0
                + (1.0 - candidate * candidate) * reset * ((1.0 - reset) * memory * d1 + d2)
            )
            offset = target - slope * previous
            gain = slope if gain is None else slope * gain
            shift_ = offset if shift_ is None else slope * shift_ + offset
            gs[n, rows, :] = gain
            ss[n, rows, :] = shift_
        for k in (1, 2, 4, 8):
            before_gain = jnp.where(sub_row < k, 1.0, pltpu.roll(gain, k, 0))
            before_shift = jnp.where(sub_row < k, 0.0, pltpu.roll(shift_, k, 0))
            shift_ = gain * before_shift + shift_
            gain = gain * before_gain
        eg[n] = jnp.where(sub_row < 1, 1.0, pltpu.roll(gain, 1, 0))
        es[n] = jnp.where(sub_row < 1, 0.0, pltpu.roll(shift_, 1, 0))
        own = slice(n * CW, (n + 1) * CW)
        total[it, 0:1, own] = gain[SUB - 1 :, :]
        total[it, 1:2, own] = shift_[SUB - 1 :, :]

    def send_totals(it):
        for away in AWAY:
            device, copy = total_to(it, away)

            @pl.when(device > tm)
            def _():
                copy.start()

    def enter_block(it):
        def receive(p, carry):
            total_from(it, p).wait_recv()
            return carry

        def join(p, state):
            return totals[it, p, 0:1, :] * state + totals[it, p, 1:2, :]

        lax.fori_loop(0, tm, receive, 0)
        mine[0:1, :] = lax.fori_loop(0, tm, join, h0[...])

    def enter_of(n):
        return eg[n] * mine[0:1, pl.ds(pl.multiple_of(n * CW, CW), CW)] + es[n]

    def loop(body, first=0, end=NC):
        def step(n, carry):
            body(n)
            return carry

        lax.fori_loop(first, end, step, 0)

    def apply_middle(n):
        enter = enter_of(n)
        hprev[n, 0:SUB, :] = enter
        xb[1, 0, n, 0:SUB, :] = enter.astype(jnp.bfloat16)
        for i in range(ROWS // SUB - 1):
            state = gs[n, tile_of(i), :] * enter + ss[n, tile_of(i), :]
            hprev[n, tile_of(i + 1), :] = state
            xb[1, 0, n, tile_of(i + 1), :] = state.astype(jnp.bfloat16)
        to_right(1, n).start()
        to_left(1, n).start()

    def store_out(n):
        cols = pl.ds(pl.multiple_of(n * CW, CW), CW)
        return pltpu.make_async_copy(outv.at[n], out.at[:, cols], out_sem.at[n])

    def apply_last(n):
        enter = enter_of(n)
        for i in range(ROWS // SUB):
            state = gs[n, tile_of(i), :] * enter + ss[n, tile_of(i), :]
            states[n, tile_of(i), :] = state.astype(jnp.bfloat16)
        outv[n] = dot(perm[0], states[n]).astype(jnp.bfloat16)
        store_out(n).start()

    for it in range(ITERS):
        if it == 0:
            load_weights(0).wait()
            same = r == t
            for n in range(NC):
                block = slice(n * CW, (n + 1) * CW)
                for g in range(3):
                    square = wv[0, g, block, block].astype(jnp.float32)
                    diag[n, g : g + 1, :] = jnp.sum(jnp.where(same, square, 0.0), axis=0, keepdims=True)
        accumulate(it, [(0, c) for c in range(NC)], True)
        for c in range(NC):
            opposite = (c + half) % NC
            to_right(it, c).wait_recv()
            to_left(it, opposite).wait_recv()
            if c < half:
                forward(it, c).start()
                forward(it, opposite).start()
            if c < half - 1:
                continue
            if c == half - 1:
                if it == 0:
                    edges[0].wait_recv()
                    edges[2].start()
                    edges[1].wait_recv()
                    edges[3].start()
                    hear(1, partner)
                    tell(2, y_pair)
                    load_weights(1).wait()
                    load_weights(3).wait()
                for k in range(half - 1):
                    accumulate(it, [(3, k), (1, k + half)])
            accumulate(it, [(3, c), (1, opposite)])
            if it == 0 and c == half:
                hear(2, y_pair)
                tell(3, y_pair)
        if it == 0:
            load_weights(2).wait()
            edges[2].wait_recv()
            edges[3].wait_recv()
            hear(3, y_pair)
        for c in range(half):
            forward(it, c).wait_recv()
            forward(it, c + half).wait_recv()
            if c < half - 1:
                accumulate(it, [(2, c), (2, c + half)])
        for n in range(NC):
            accumulate(it, [(2, half - 1), (2, NC - 1)], parts=[n])
            if n > 0:
                gates(it, n - 1)
        gates(it, NC - 1)
        send_totals(it)
        enter_block(it)
        loop(apply_middle if it == 0 else apply_last)

    boundary.wait_send()
    for copy in edges:
        copy.wait_send()
    for it in range(ITERS):
        for c in range(NC):
            to_right(it, c).wait_send()
            to_left(it, c).wait_send()
            forward(it, c).wait_send()

        for away in AWAY:
            device, copy = total_to(it, away)

            @pl.when(device > tm)
            def _():
                copy.wait_send()

    loop(lambda n: store_out(n).wait())


def per_device(gate_inputs, recurrent, initial_state, guess):
    bf16, f32 = jnp.bfloat16, jnp.float32
    dma = pltpu.SemaphoreType.DMA
    hbm = pl.BlockSpec(memory_space=pl.ANY)
    vmem = pl.BlockSpec(memory_space=pltpu.VMEM)
    return pl.pallas_call(
        kernel,
        out_shape=jax.ShapeDtypeStruct((ROWS, UNITS), bf16),
        in_specs=[hbm, hbm, vmem, hbm],
        out_specs=hbm,
        scratch_shapes=[
            pltpu.VMEM((4, 3, UNITS, UNITS), bf16),
            pltpu.VMEM((3, ROWS, UNITS), bf16),
            pltpu.VMEM((ROWS, UNITS), bf16),
            pltpu.VMEM((ITERS, 4, NC, ROWS, CW), bf16),
            pltpu.VMEM((NC, 3, ROWS, CW), f32),
            pltpu.VMEM((NC, 3, ROWS, CW), f32),
            pltpu.VMEM((NC, ROWS, CW), f32),
            pltpu.VMEM((NC, ROWS, CW), f32),
            pltpu.VMEM((NC, ROWS, CW), f32),
            pltpu.VMEM((NC, SUB, CW), f32),
            pltpu.VMEM((NC, SUB, CW), f32),
            pltpu.VMEM((NC, 8, CW), f32),
            pltpu.VMEM((SUB, UNITS), bf16),
            pltpu.VMEM((ITERS, 2, UNITS), f32),
            pltpu.VMEM((ITERS, STEPS, 2, UNITS), f32),
            pltpu.VMEM((8, UNITS), f32),
            pltpu.VMEM((2, ROWS, ROWS), bf16),
            pltpu.VMEM((NC, ROWS, CW), bf16),
            pltpu.VMEM((NC, ROWS, CW), bf16),
            dma((2,)),
            dma((4,)),
            dma((NC,)),
            dma((2,)),
            dma((ITERS, NC)),
            dma((ITERS, NC)),
            dma((ITERS, NC)),
            dma((ITERS, 4, NC)),
            dma((4,)),
            dma((4,)),
            dma((ITERS, STEPS)),
            dma((ITERS, STEPS)),
            pltpu.SemaphoreType.REGULAR((4,)),
        ],
        compiler_params=pltpu.CompilerParams(
            collective_id=0, has_side_effects=True, vmem_limit_bytes=58 * 2**20
        ),
    )(jnp.transpose(gate_inputs, (1, 0, 2)), recurrent, initial_state[None, :], guess)


def solution(mesh):
    in_specs = (P("tm", None, "hid"), P(None, None, "hid"), P("hid"), P("tm", "hid"))
    return jax.shard_map(
        per_device, mesh=mesh, in_specs=in_specs, out_specs=P("tm", "hid"), check_vma=False
    )
```

```python
import jax
import jax.numpy as jnp
from jax import lax
from jax.experimental import pallas as pl
from jax.experimental.pallas import tpu as pltpu
from jax.sharding import PartitionSpec as P

ITERS = 2
ROWS = 256
UNITS = 1024
SUB = 16
CW = 256
NC = UNITS // CW
GROUP = 8
LINES = 4
LANES = 128
ZC = UNITS // LANES
XS = 4
STEPS = GROUP * LINES
AWAY = sorted(
    [(a, b, c) for a in range(LINES) for b in range(XS) for c in range(2) if (a, b, c) != (0, 0, 0)],
    key=lambda k: -(min(k[0], LINES - k[0]) + min(k[1], XS - k[1])),
)
MESH = pl.DeviceIdType.MESH


def dot(a, b):
    return jnp.dot(a, b, preferred_element_type=jnp.float32)


def sigmoid(x):
    return 0.5 * jnp.tanh(0.5 * x) + 0.5


def kernel(
    gi, w, h0, guess, out,
    wv, giv, gv, xb, acc, ip, hprev, gs, ss, eg, es, diag, last, edge, top, total, totals, mine, perm, states, outv,
    load_sem, w_sem, out_sem, last_sem, right_s, left_s, fwd_s, z_r, edge_s, edge_r, t_s, t_r, known,
):
    tm = lax.axis_index("tm")
    z = lax.axis_index("hid")
    y, q = tm // GROUP, lax.rem(tm, GROUP)
    right, left = lax.rem(z + 1, 4), lax.rem(z + 3, 4)

    load_guess = pltpu.make_async_copy(guess, gv, load_sem.at[0])
    load_inputs = pltpu.make_async_copy(gi, giv, load_sem.at[1])

    def load_weights(d):
        rows = pl.ds(pl.multiple_of(lax.rem(z + d, 4) * UNITS, UNITS), UNITS)
        return pltpu.make_async_copy(w.at[:, rows, :], wv.at[d], w_sem.at[d])

    load_guess.start()
    load_weights(0).start()
    load_inputs.start()
    load_weights(1).start()
    load_weights(3).start()

    barrier = pltpu.get_barrier_semaphore()

    def greet(device):
        pl.semaphore_signal(barrier, inc=1, device_id=device, device_id_type=MESH)

    x, core = q // 2, lax.rem(q, 2)

    def device_at(a, b, c):
        return lax.rem(y + a, LINES) * GROUP + lax.rem(x + b, XS) * 2 + lax.rem(core + c, 2)

    x_pair = ((device_at(0, 1, 0), z), (device_at(0, XS - 1, 0), z))
    y_pair = ((device_at(1, 0, 0), z), (device_at(LINES - 1, 0, 0), z))
    partner = ((device_at(0, 0, 1), z),)
    later = (lax.rem(tm + 1, STEPS), z)
    earlier = (lax.rem(tm + STEPS - 1, STEPS), z)
    near = ((tm, right), (tm, left), later, earlier) + x_pair + y_pair + partner
    for device in near:
        greet(device)

    r = lax.broadcasted_iota(jnp.int32, (ROWS, ROWS), 0)
    t = lax.broadcasted_iota(jnp.int32, (ROWS, ROWS), 1)
    time = (r & (SUB - 1)) * SUB + (r >> 4)
    perm[0] = jnp.where(t == time, 1.0, 0.0).astype(jnp.bfloat16)
    perm[1] = jnp.where(t == time - 1, 1.0, 0.0).astype(jnp.bfloat16)

    load_guess.wait()

    last[0] = gv[ROWS - SUB :, :].astype(jnp.float32)[SUB - 1 :, :]
    for n in range(NC):
        rows = dot(perm[1], gv[:, n * CW : (n + 1) * CW])
        hprev[n] = rows
        for k in range(2):
            xb[0, 0, 2 * n + k] = rows[:, k * LANES : (k + 1) * LANES].astype(jnp.bfloat16)

    pl.semaphore_wait(barrier, len(near))

    def remote(src, dst, send, recv, device):
        return pltpu.make_async_remote_copy(
            src_ref=src, dst_ref=dst, send_sem=send, recv_sem=recv, device_id=device, device_id_type=MESH
        )

    half = NC // 2

    def part(it, d, m):
        return xb.at[it, d, pl.ds(2 * m, 2)]

    def to_right(it, m):
        return remote(part(it, 0, m), part(it, 3, m), right_s.at[it, m], z_r.at[it, 0, m], (tm, right))

    def to_left(it, m):
        return remote(part(it, 0, m), part(it, 1, m), left_s.at[it, m], z_r.at[it, 1, m], (tm, left))

    def forward(it, c, size):
        src, device = (3, right) if c < ZC // 2 else (1, left)
        here, there = xb.at[it, src, pl.ds(c, size)], xb.at[it, 2, pl.ds(c, size)]
        return remote(here, there, fwd_s.at[it, c], z_r.at[it, 2, c], (tm, device))

    boundary = remote(last.at[0], last.at[1], last_sem.at[0], last_sem.at[1], later)
    edges = (
        remote(edge.at[0], edge.at[3], edge_s.at[0], edge_r.at[0], (tm, right)),
        remote(edge.at[0], edge.at[1], edge_s.at[1], edge_r.at[1], (tm, left)),
        remote(edge.at[3], edge.at[2], edge_s.at[2], edge_r.at[2], (tm, right)),
    )

    boundary.start()
    for m in range(half):
        to_right(0, m).start()
        to_left(0, half + m).start()

    def tell(k, devices):
        for device in devices:
            pl.semaphore_signal(known.at[k], inc=1, device_id=device, device_id_type=MESH)

    def hear(k, devices):
        pl.semaphore_wait(known.at[k], len(devices))

    tell(0, x_pair)
    boundary.wait_recv()
    first = lax.broadcasted_iota(jnp.int32, (SUB, LANES), 0) == 0
    for c in range(ZC):
        cols = slice(c * LANES, (c + 1) * LANES)
        edge[0, :, cols] = jnp.where(tm == 0, h0[c : c + 1, :], last[1, :, cols])
    edges[0].start()
    edges[1].start()
    for m in range(half):
        to_right(0, half + m).start()
        to_left(0, m).start()
    for n in range(NC):
        for k in range(2):
            lanes = slice(k * LANES, (k + 1) * LANES)
            row = edge[0, :, n * CW + k * LANES : n * CW + (k + 1) * LANES]
            hprev[n, 0:SUB, lanes] = jnp.where(first, row, hprev[n, 0:SUB, lanes])

    def set_edge(d, pieces):
        for c in pieces:
            row = edge[d, :, c * LANES : (c + 1) * LANES]
            tile = xb[0, d, c, 0:SUB, :].astype(jnp.float32)
            top[d, c] = jnp.where(first, row, tile).astype(jnp.bfloat16)

    hear(0, x_pair)
    tell(1, partner)

    load_inputs.wait()

    for n in range(NC):
        for g in range(3):
            ip[n, g] = dot(perm[0], giv[g, :, n * CW : (n + 1) * CW])

    def block_piece(it, d, c):
        if it > 0:
            return xb[it, d, c]
        return jnp.concatenate([top[d, c], xb[it, d, c, SUB:, :]], axis=0)

    def accumulate(it, pieces, start=False, parts=range(NC)):
        for n in parts:
            cols = slice(n * CW, (n + 1) * CW)
            for g in range(3):
                terms = None if start else acc[n, g]
                for pair in zip(pieces[0::2], pieces[1::2]):
                    rows = jnp.concatenate([block_piece(it, d, c) for d, c in pair], axis=1)
                    (d0, c0), (d1, c1) = pair
                    if (d0, c0 + 1) == (d1, c1):
                        weights = wv[d0, g, c0 * LANES : (c0 + 2) * LANES, cols]
                    else:
                        weights = jnp.concatenate(
                            [wv[d, g, c * LANES : (c + 1) * LANES, cols] for d, c in pair], axis=0
                        )
                    term = dot(rows, weights)
                    terms = term if terms is None else terms + term
                acc[n, g] = terms

    sub_row = lax.broadcasted_iota(jnp.int32, (SUB, CW), 0)

    def tile_of(i):
        return slice(i * SUB, (i + 1) * SUB)

    def total_to(it, away):
        device = device_at(*away)
        copy = remote(total.at[it], totals.at[it, tm], t_s.at[it, device], t_r.at[it, tm], (device, z))
        return device, copy

    def total_from(it, p):
        return remote(total.at[it], totals.at[it, p], t_s.at[it, p], t_r.at[it, p], (tm, right))

    def gates(it, n):
        d0, d1, d2 = (jnp.broadcast_to(diag[n, g : g + 1, :], (SUB, CW)) for g in range(3))
        gain = shift_ = None
        for i in range(ROWS // SUB):
            rows = tile_of(i)
            previous = hprev[n, rows, :]
            memory = acc[n, 2, rows, :]
            update = sigmoid(ip[n, 0, rows, :] + acc[n, 0, rows, :])
            reset = sigmoid(ip[n, 1, rows, :] + acc[n, 1, rows, :])
            candidate = jnp.tanh(ip[n, 2, rows, :] + reset * memory)
            keep = 1.0 - update
            gap = previous - candidate
            target = candidate + update * gap
            slope = update + keep * (
                update * gap * d0
                + (1.0 - candidate * candidate) * reset * ((1.0 - reset) * memory * d1 + d2)
            )
            offset = target - slope * previous
            gain = slope if gain is None else slope * gain
            shift_ = offset if shift_ is None else slope * shift_ + offset
            gs[n, rows, :] = gain
            ss[n, rows, :] = shift_
        for k in (1, 2, 4, 8):
            before_gain = jnp.where(sub_row < k, 1.0, pltpu.roll(gain, k, 0))
            before_shift = jnp.where(sub_row < k, 0.0, pltpu.roll(shift_, k, 0))
            shift_ = gain * before_shift + shift_
            gain = gain * before_gain
        eg[n] = jnp.where(sub_row < 1, 1.0, pltpu.roll(gain, 1, 0))
        es[n] = jnp.where(sub_row < 1, 0.0, pltpu.roll(shift_, 1, 0))
        for k in range(2):
            lanes = slice(k * LANES, (k + 1) * LANES)
            row = slice(2 * n + k, 2 * n + k + 1)
            total[it, 0, row, :] = gain[SUB - 1 :, lanes]
            total[it, 1, row, :] = shift_[SUB - 1 :, lanes]

    def send_totals(it):
        for away in AWAY:
            device, copy = total_to(it, away)

            @pl.when(device > tm)
            def _():
                copy.start()

    def enter_block(it):
        def join(p, state):
            total_from(it, p).wait_recv()
            return totals[it, p, 0] * state + totals[it, p, 1]

        mine[...] = lax.fori_loop(0, tm, join, h0[...])

    def enter_of(n):
        row = jnp.concatenate([mine[2 * n : 2 * n + 1, :], mine[2 * n + 1 : 2 * n + 2, :]], axis=1)
        return eg[n] * row + es[n]

    def apply_middle(n):
        enter = enter_of(n)
        hprev[n, 0:SUB, :] = enter
        for k in range(2):
            lanes = slice(k * LANES, (k + 1) * LANES)
            xb[1, 0, 2 * n + k, 0:SUB, :] = enter[:, lanes].astype(jnp.bfloat16)
        for i in range(ROWS // SUB - 1):
            state = gs[n, tile_of(i), :] * enter + ss[n, tile_of(i), :]
            hprev[n, tile_of(i + 1), :] = state
            for k in range(2):
                lanes = slice(k * LANES, (k + 1) * LANES)
                xb[1, 0, 2 * n + k, tile_of(i + 1), :] = state[:, lanes].astype(jnp.bfloat16)
        to_right(1, n).start()
        to_left(1, n).start()

    def store_out(n):
        return pltpu.make_async_copy(outv.at[n], out.at[:, pl.ds(n * CW, CW)], out_sem.at[n])

    def apply_last(n):
        enter = enter_of(n)
        for i in range(ROWS // SUB):
            state = gs[n, tile_of(i), :] * enter + ss[n, tile_of(i), :]
            states[n, tile_of(i), :] = state.astype(jnp.bfloat16)
        outv[n] = dot(perm[0], states[n]).astype(jnp.bfloat16)
        store_out(n).start()

    for it in range(ITERS):
        if it == 0:
            load_weights(0).wait()
            same = r == t
            for n in range(NC):
                block = slice(n * CW, (n + 1) * CW)
                for g in range(3):
                    square = wv[0, g, block, block].astype(jnp.float32)
                    diag[n, g : g + 1, :] = jnp.sum(jnp.where(same, square, 0.0), axis=0, keepdims=True)
            set_edge(0, range(ZC))
        accumulate(it, [(0, c) for c in range(ZC)], True)
        for m in range(NC):
            opposite = (m + half) % NC
            to_right(it, m).wait_recv()
            to_left(it, opposite).wait_recv()
            if m == 0:
                forward(it, 0, 2).start()
                forward(it, 4, 2).start()
                if it == 0:
                    load_weights(2).start()
                continue
            fresh = [(3, 2 * m), (3, 2 * m + 1), (1, 2 * opposite), (1, 2 * opposite + 1)]
            if m == 1:
                if it == 0:
                    edges[0].wait_recv()
                    edges[2].start()
                for c in (2, 6, 3, 7):
                    forward(it, c, 1).start()
                fresh = [(3, 0), (3, 1), (1, 4), (1, 5)] + fresh
                if it == 0:
                    edges[1].wait_recv()
                    hear(1, partner)
                    tell(2, y_pair)
                    load_weights(1).wait()
                    load_weights(3).wait()
            if it == 0:
                for d, c in fresh:
                    set_edge(d, [c])
            accumulate(it, fresh)
            if it == 0 and m == half:
                hear(2, y_pair)
                tell(3, y_pair)
        if it == 0:
            load_weights(2).wait()
            edges[2].wait_recv()
            hear(3, y_pair)
        for c, size in ((0, 2), (2, 1), (3, 1)):
            forward(it, c, size).wait_recv()
            forward(it, c + ZC // 2, size).wait_recv()
            fresh = [(2, c + k) for k in range(size)] + [(2, c + ZC // 2 + k) for k in range(size)]
            if it == 0:
                for d, k in fresh:
                    set_edge(d, [k])
            if c < 3:
                accumulate(it, fresh)
        for n in range(NC):
            accumulate(it, fresh, parts=[n])
            if n > 0:
                gates(it, n - 1)
        gates(it, NC - 1)
        send_totals(it)
        enter_block(it)
        for n in range(NC):
            (apply_middle if it == 0 else apply_last)(n)

    boundary.wait_send()
    for copy in edges:
        copy.wait_send()
    for it in range(ITERS):
        for m in range(NC):
            to_right(it, m).wait_send()
            to_left(it, m).wait_send()
        for c, size in ((0, 2), (2, 1), (3, 1)):
            forward(it, c, size).wait_send()
            forward(it, c + ZC // 2, size).wait_send()
        for away in AWAY:
            device, copy = total_to(it, away)

            @pl.when(device > tm)
            def _():
                copy.wait_send()

    for n in range(NC):
        store_out(n).wait()


def per_device(gate_inputs, recurrent, initial_state, guess):
    bf16, f32 = jnp.bfloat16, jnp.float32
    dma = pltpu.SemaphoreType.DMA
    hbm = pl.BlockSpec(memory_space=pl.ANY)
    vmem = pl.BlockSpec(memory_space=pltpu.VMEM)
    return pl.pallas_call(
        kernel,
        out_shape=jax.ShapeDtypeStruct((ROWS, UNITS), bf16),
        in_specs=[hbm, hbm, vmem, hbm],
        out_specs=hbm,
        scratch_shapes=[
            pltpu.VMEM((4, 3, UNITS, UNITS), bf16),
            pltpu.VMEM((3, ROWS, UNITS), bf16),
            pltpu.VMEM((ROWS, UNITS), bf16),
            pltpu.VMEM((ITERS, 4, ZC, ROWS, LANES), bf16),
            pltpu.VMEM((NC, 3, ROWS, CW), f32),
            pltpu.VMEM((NC, 3, ROWS, CW), f32),
            pltpu.VMEM((NC, ROWS, CW), f32),
            pltpu.VMEM((NC, ROWS, CW), f32),
            pltpu.VMEM((NC, ROWS, CW), f32),
            pltpu.VMEM((NC, SUB, CW), f32),
            pltpu.VMEM((NC, SUB, CW), f32),
            pltpu.VMEM((NC, 8, CW), f32),
            pltpu.VMEM((2, 1, UNITS), f32),
            pltpu.VMEM((4, 1, UNITS), f32),
            pltpu.VMEM((4, ZC, SUB, LANES), bf16),
            pltpu.VMEM((ITERS, 2, 8, LANES), f32),
            pltpu.VMEM((ITERS, STEPS, 2, 8, LANES), f32),
            pltpu.VMEM((8, LANES), f32),
            pltpu.VMEM((2, ROWS, ROWS), bf16),
            pltpu.VMEM((NC, ROWS, CW), bf16),
            pltpu.VMEM((NC, ROWS, CW), bf16),
            dma((2,)),
            dma((4,)),
            dma((NC,)),
            dma((2,)),
            dma((ITERS, NC)),
            dma((ITERS, NC)),
            dma((ITERS, ZC)),
            dma((ITERS, 3, ZC)),
            dma((3,)),
            dma((3,)),
            dma((ITERS, STEPS)),
            dma((ITERS, STEPS)),
            pltpu.SemaphoreType.REGULAR((4,)),
        ],
        compiler_params=pltpu.CompilerParams(
            collective_id=0, has_side_effects=True, vmem_limit_bytes=58 * 2**20
        ),
    )(jnp.transpose(gate_inputs, (1, 0, 2)), recurrent, initial_state.reshape(8, LANES), guess)


def solution(mesh):
    in_specs = (P("tm", None, "hid"), P(None, None, "hid"), P("hid"), P("tm", "hid"))
    return jax.shard_map(
        per_device, mesh=mesh, in_specs=in_specs, out_specs=P("tm", "hid"), check_vma=False
    )
```

```python
import jax
import jax.numpy as jnp
from jax import lax
from jax.experimental import pallas as pl
from jax.experimental.pallas import tpu as pltpu
from jax.sharding import PartitionSpec as P

ITERS = 2
ROWS = 256
UNITS = 1024
SUB = 16
CW = 256
NC = UNITS // CW
GROUP = 8
LINES = 4
LANES = 128
ZC = UNITS // LANES
XS = 4
STEPS = GROUP * LINES
AWAY = sorted(
    [(a, b, c) for a in range(LINES) for b in range(XS) for c in range(2) if (a, b, c) != (0, 0, 0)],
    key=lambda k: -(min(k[0], LINES - k[0]) + min(k[1], XS - k[1])),
)
MESH = pl.DeviceIdType.MESH


def dot(a, b):
    return jnp.dot(a, b, preferred_element_type=jnp.float32)


def sigmoid(x):
    return 0.5 * jnp.tanh(0.5 * x) + 0.5


def kernel(
    gi, w, h0, guess, out,
    wv, giv, gv, xb, acc, ip, hprev, gs, ss, eg, es, diag, last, edge, top, total, totals, mine, perm, states, outv, terms_own, terms_got, enters,
    load_sem, w_sem, out_sem, last_sem, right_s, left_s, fwd_s, z_r, edge_s, edge_r, t_s, t_r, known, terms_s, terms_r, enters_s, enters_r,
):
    tm = lax.axis_index("tm")
    z = lax.axis_index("hid")
    y, q = tm // GROUP, lax.rem(tm, GROUP)
    right, left = lax.rem(z + 1, 4), lax.rem(z + 3, 4)

    load_guess = pltpu.make_async_copy(guess, gv, load_sem.at[0])
    load_inputs = pltpu.make_async_copy(gi, giv, load_sem.at[1])

    def load_weights(d):
        rows = pl.ds(pl.multiple_of(lax.rem(z + d, 4) * UNITS, UNITS), UNITS)
        return pltpu.make_async_copy(w.at[:, rows, :], wv.at[d], w_sem.at[d])

    load_guess.start()
    load_weights(0).start()
    load_inputs.start()
    load_weights(1).start()
    load_weights(3).start()

    barrier = pltpu.get_barrier_semaphore()

    def greet(device):
        pl.semaphore_signal(barrier, inc=1, device_id=device, device_id_type=MESH)

    x, core = q // 2, lax.rem(q, 2)

    def device_at(a, b, c):
        return lax.rem(y + a, LINES) * GROUP + lax.rem(x + b, XS) * 2 + lax.rem(core + c, 2)

    x_pair = ((device_at(0, 1, 0), z), (device_at(0, XS - 1, 0), z))
    y_pair = ((device_at(1, 0, 0), z), (device_at(LINES - 1, 0, 0), z))
    partner = ((device_at(0, 0, 1), z),)
    later = (lax.rem(tm + 1, STEPS), z)
    earlier = (lax.rem(tm + STEPS - 1, STEPS), z)
    near = ((tm, right), (tm, left), later, earlier) + x_pair + y_pair + partner
    for device in near:
        greet(device)

    r = lax.broadcasted_iota(jnp.int32, (ROWS, ROWS), 0)
    t = lax.broadcasted_iota(jnp.int32, (ROWS, ROWS), 1)
    time = (r & (SUB - 1)) * SUB + (r >> 4)
    perm[0] = jnp.where(t == time, 1.0, 0.0).astype(jnp.bfloat16)
    perm[1] = jnp.where(t == time - 1, 1.0, 0.0).astype(jnp.bfloat16)

    load_guess.wait()

    last[0] = gv[ROWS - SUB :, :].astype(jnp.float32)[SUB - 1 :, :]
    for n in range(NC):
        rows = dot(perm[1], gv[:, n * CW : (n + 1) * CW])
        hprev[n] = rows
        for k in range(2):
            xb[0, 0, 2 * n + k] = rows[:, k * LANES : (k + 1) * LANES].astype(jnp.bfloat16)

    pl.semaphore_wait(barrier, len(near))

    def remote(src, dst, send, recv, device):
        return pltpu.make_async_remote_copy(
            src_ref=src, dst_ref=dst, send_sem=send, recv_sem=recv, device_id=device, device_id_type=MESH
        )

    half = NC // 2

    def part(it, d, m):
        return xb.at[it, d, pl.ds(2 * m, 2)]

    def to_right(it, m):
        return remote(part(it, 0, m), part(it, 3, m), right_s.at[it, m], z_r.at[it, 0, m], (tm, right))

    def to_left(it, m):
        return remote(part(it, 0, m), part(it, 1, m), left_s.at[it, m], z_r.at[it, 1, m], (tm, left))

    def forward(it, c, size):
        src, device = (3, right) if c < ZC // 2 else (1, left)
        here, there = xb.at[it, src, pl.ds(c, size)], xb.at[it, 2, pl.ds(c, size)]
        return remote(here, there, fwd_s.at[it, c], z_r.at[it, 2, c], (tm, device))

    boundary = remote(last.at[0], last.at[1], last_sem.at[0], last_sem.at[1], later)
    edges = (
        remote(edge.at[0], edge.at[3], edge_s.at[0], edge_r.at[0], (tm, right)),
        remote(edge.at[0], edge.at[1], edge_s.at[1], edge_r.at[1], (tm, left)),
        remote(edge.at[3], edge.at[2], edge_s.at[2], edge_r.at[2], (tm, right)),
    )

    sides = ((tm, right), (tm, left))
    terms_out = [
        remote(terms_own, terms_got.at[k], terms_s.at[k], terms_r.at[k], sides[k]) for k in range(2)
    ]
    enters_out = [
        remote(enters.at[2], enters.at[k], enters_s.at[k], enters_r.at[k], sides[k]) for k in range(2)
    ]

    boundary.start()
    for m in range(half):
        to_right(0, m).start()
        to_left(0, half + m).start()

    def tell(k, devices):
        for device in devices:
            pl.semaphore_signal(known.at[k], inc=1, device_id=device, device_id_type=MESH)

    def hear(k, devices):
        pl.semaphore_wait(known.at[k], len(devices))

    tell(0, x_pair)
    boundary.wait_recv()
    first = lax.broadcasted_iota(jnp.int32, (SUB, LANES), 0) == 0
    for c in range(ZC):
        cols = slice(c * LANES, (c + 1) * LANES)
        edge[0, :, cols] = jnp.where(tm == 0, h0[c : c + 1, :], last[1, :, cols])
    edges[0].start()
    edges[1].start()
    for m in range(half):
        to_right(0, half + m).start()
        to_left(0, m).start()
    for n in range(NC):
        for k in range(2):
            lanes = slice(k * LANES, (k + 1) * LANES)
            row = edge[0, :, n * CW + k * LANES : n * CW + (k + 1) * LANES]
            hprev[n, 0:SUB, lanes] = jnp.where(first, row, hprev[n, 0:SUB, lanes])

    def set_edge(d, pieces):
        for c in pieces:
            row = edge[d, :, c * LANES : (c + 1) * LANES]
            tile = xb[0, d, c, 0:SUB, :].astype(jnp.float32)
            top[d, c] = jnp.where(first, row, tile).astype(jnp.bfloat16)

    hear(0, x_pair)
    tell(1, partner)

    load_inputs.wait()

    for n in range(NC):
        for g in range(3):
            ip[n, g] = dot(perm[0], giv[g, :, n * CW : (n + 1) * CW])

    def block_piece(it, d, c):
        if it > 0:
            return xb[it, d, c]
        return jnp.concatenate([top[d, c], xb[it, d, c, SUB:, :]], axis=0)

    def accumulate(it, pieces, start=False, parts=range(NC)):
        for n in parts:
            cols = slice(n * CW, (n + 1) * CW)
            for g in range(3):
                terms = None if start else acc[n, g]
                for pair in zip(pieces[0::2], pieces[1::2]):
                    rows = jnp.concatenate([block_piece(it, d, c) for d, c in pair], axis=1)
                    (d0, c0), (d1, c1) = pair
                    if (d0, c0 + 1) == (d1, c1):
                        weights = wv[d0, g, c0 * LANES : (c0 + 2) * LANES, cols]
                    else:
                        weights = jnp.concatenate(
                            [wv[d, g, c * LANES : (c + 1) * LANES, cols] for d, c in pair], axis=0
                        )
                    term = dot(rows, weights)
                    terms = term if terms is None else terms + term
                acc[n, g] = terms

    sub_row = lax.broadcasted_iota(jnp.int32, (SUB, CW), 0)

    def tile_of(i):
        return slice(i * SUB, (i + 1) * SUB)

    def total_to(it, away):
        device = device_at(*away)
        copy = remote(total.at[it], totals.at[it, tm], t_s.at[it, device], t_r.at[it, tm], (device, z))
        return device, copy

    def total_from(it, p):
        return remote(total.at[it], totals.at[it, p], t_s.at[it, p], t_r.at[it, p], (tm, right))

    def gates(it, n):
        d0, d1, d2 = (jnp.broadcast_to(diag[n, g : g + 1, :], (SUB, CW)) for g in range(3))
        gain = shift_ = None
        for i in range(ROWS // SUB):
            rows = tile_of(i)
            previous = hprev[n, rows, :]
            memory = acc[n, 2, rows, :]
            update = sigmoid(ip[n, 0, rows, :] + acc[n, 0, rows, :])
            reset = sigmoid(ip[n, 1, rows, :] + acc[n, 1, rows, :])
            candidate = jnp.tanh(ip[n, 2, rows, :] + reset * memory)
            keep = 1.0 - update
            gap = previous - candidate
            target = candidate + update * gap
            slope = update + keep * (
                update * gap * d0
                + (1.0 - candidate * candidate) * reset * ((1.0 - reset) * memory * d1 + d2)
            )
            offset = target - slope * previous
            gain = slope if gain is None else slope * gain
            shift_ = offset if shift_ is None else slope * shift_ + offset
            gs[n, rows, :] = gain
            ss[n, rows, :] = shift_
            if it == 0 and n == 0 and i < ROWS // SUB - 1:
                for k in range(2):
                    lanes = slice(k * LANES, (k + 1) * LANES)
                    terms_own[0, k, rows, :] = gain[:, lanes].astype(jnp.bfloat16)
                    terms_own[1, k, rows, :] = shift_[:, lanes].astype(jnp.bfloat16)
        for k in (1, 2, 4, 8):
            before_gain = jnp.where(sub_row < k, 1.0, pltpu.roll(gain, k, 0))
            before_shift = jnp.where(sub_row < k, 0.0, pltpu.roll(shift_, k, 0))
            shift_ = gain * before_shift + shift_
            gain = gain * before_gain
        eg[n] = jnp.where(sub_row < 1, 1.0, pltpu.roll(gain, 1, 0))
        es[n] = jnp.where(sub_row < 1, 0.0, pltpu.roll(shift_, 1, 0))
        for k in range(2):
            lanes = slice(k * LANES, (k + 1) * LANES)
            row = slice(2 * n + k, 2 * n + k + 1)
            total[it, 0, row, :] = gain[SUB - 1 :, lanes]
            total[it, 1, row, :] = shift_[SUB - 1 :, lanes]

    def send_totals(it):
        for away in AWAY:
            device, copy = total_to(it, away)

            @pl.when(device > tm)
            def _():
                copy.start()

    def enter_block(it):
        def join(p, state):
            total_from(it, p).wait_recv()
            return totals[it, p, 0] * state + totals[it, p, 1]

        mine[...] = lax.fori_loop(0, tm, join, h0[...])

    def enter_of(n):
        row = jnp.concatenate([mine[2 * n : 2 * n + 1, :], mine[2 * n + 1 : 2 * n + 2, :]], axis=1)
        return eg[n] * row + es[n]

    def apply_middle(n):
        enter = enter_of(n)
        hprev[n, 0:SUB, :] = enter
        for k in range(2):
            lanes = slice(k * LANES, (k + 1) * LANES)
            xb[1, 0, 2 * n + k, 0:SUB, :] = enter[:, lanes].astype(jnp.bfloat16)
        for i in range(ROWS // SUB - 1):
            state = gs[n, tile_of(i), :] * enter + ss[n, tile_of(i), :]
            hprev[n, tile_of(i + 1), :] = state
            for k in range(2):
                lanes = slice(k * LANES, (k + 1) * LANES)
                xb[1, 0, 2 * n + k, tile_of(i + 1), :] = state[:, lanes].astype(jnp.bfloat16)
        if n == 0:
            for k in range(2):
                enters[2, k] = enter[:, k * LANES : (k + 1) * LANES]
            for copy in enters_out:
                copy.start()
        else:
            to_right(1, n).start()
            to_left(1, n).start()

    def join_terms(k, d):
        terms_out[k].wait_recv()
        enters_out[k].wait_recv()
        for j in range(2):
            enter = enters[k, j]
            xb[1, d, j, 0:SUB, :] = enter.astype(jnp.bfloat16)
            for i in range(ROWS // SUB - 1):
                gain = terms_got[k, 0, j, tile_of(i), :].astype(jnp.float32)
                shift_ = terms_got[k, 1, j, tile_of(i), :].astype(jnp.float32)
                xb[1, d, j, tile_of(i + 1), :] = (gain * enter + shift_).astype(jnp.bfloat16)

    def store_out(n):
        return pltpu.make_async_copy(outv.at[n], out.at[:, pl.ds(n * CW, CW)], out_sem.at[n])

    def apply_last(n):
        enter = enter_of(n)
        for i in range(ROWS // SUB):
            state = gs[n, tile_of(i), :] * enter + ss[n, tile_of(i), :]
            states[n, tile_of(i), :] = state.astype(jnp.bfloat16)
        outv[n] = dot(perm[0], states[n]).astype(jnp.bfloat16)
        store_out(n).start()

    for it in range(ITERS):
        if it == 0:
            load_weights(0).wait()
            same = r == t
            for n in range(NC):
                block = slice(n * CW, (n + 1) * CW)
                for g in range(3):
                    square = wv[0, g, block, block].astype(jnp.float32)
                    diag[n, g : g + 1, :] = jnp.sum(jnp.where(same, square, 0.0), axis=0, keepdims=True)
            set_edge(0, range(ZC))
        accumulate(it, [(0, c) for c in range(ZC)], True)
        if it == 1:
            join_terms(0, 3)
            forward(it, 0, 2).start()
            join_terms(1, 1)
            accumulate(it, [(3, 0), (3, 1), (1, 0), (1, 1)])
            for m in range(1, NC):
                to_right(it, m).wait_recv()
                to_left(it, m).wait_recv()
                if m == 1:
                    forward(it, 2, 1).start()
                    forward(it, 3, 1).start()
                elif m == 2:
                    forward(it, 4, 2).start()
                else:
                    forward(it, 6, 1).start()
                    forward(it, 7, 1).start()
                accumulate(it, [(d, 2 * m + k) for d in (3, 1) for k in range(2)])
        for m in range(NC if it == 0 else 0):
            opposite = (m + half) % NC
            to_right(it, m).wait_recv()
            to_left(it, opposite).wait_recv()
            if m == 0:
                forward(it, 0, 2).start()
                forward(it, 4, 2).start()
                if it == 0:
                    load_weights(2).start()
                continue
            fresh = [(3, 2 * m), (3, 2 * m + 1), (1, 2 * opposite), (1, 2 * opposite + 1)]
            if m == 1:
                if it == 0:
                    edges[0].wait_recv()
                    edges[2].start()
                for c in (2, 6, 3, 7):
                    forward(it, c, 1).start()
                fresh = [(3, 0), (3, 1), (1, 4), (1, 5)] + fresh
                if it == 0:
                    edges[1].wait_recv()
                    hear(1, partner)
                    tell(2, y_pair)
                    load_weights(1).wait()
                    load_weights(3).wait()
            if it == 0:
                for d, c in fresh:
                    set_edge(d, [c])
            accumulate(it, fresh)
            if it == 0 and m == half:
                hear(2, y_pair)
                tell(3, y_pair)
        if it == 0:
            load_weights(2).wait()
            edges[2].wait_recv()
            hear(3, y_pair)
        for c, size in ((0, 2), (2, 1), (3, 1)):
            forward(it, c, size).wait_recv()
            forward(it, c + ZC // 2, size).wait_recv()
            fresh = [(2, c + k) for k in range(size)] + [(2, c + ZC // 2 + k) for k in range(size)]
            if it == 0:
                for d, k in fresh:
                    set_edge(d, [k])
            if c < 3:
                accumulate(it, fresh)
        for n in range(NC):
            accumulate(it, fresh, parts=[n])
            if n > 0:
                gates(it, n - 1)
            if it == 0 and n == 1:
                for copy in terms_out:
                    copy.start()
        gates(it, NC - 1)
        send_totals(it)
        enter_block(it)
        for n in range(NC):
            (apply_middle if it == 0 else apply_last)(n)

    boundary.wait_send()
    for copy in terms_out + enters_out:
        copy.wait_send()
    for copy in edges:
        copy.wait_send()
    for it in range(ITERS):
        for m in range(it, NC):
            to_right(it, m).wait_send()
            to_left(it, m).wait_send()
        for c, size in ((0, 2), (2, 1), (3, 1)):
            forward(it, c, size).wait_send()
            forward(it, c + ZC // 2, size).wait_send()
        for away in AWAY:
            device, copy = total_to(it, away)

            @pl.when(device > tm)
            def _():
                copy.wait_send()

    for n in range(NC):
        store_out(n).wait()


def per_device(gate_inputs, recurrent, initial_state, guess):
    bf16, f32 = jnp.bfloat16, jnp.float32
    dma = pltpu.SemaphoreType.DMA
    hbm = pl.BlockSpec(memory_space=pl.ANY)
    vmem = pl.BlockSpec(memory_space=pltpu.VMEM)
    return pl.pallas_call(
        kernel,
        out_shape=jax.ShapeDtypeStruct((ROWS, UNITS), bf16),
        in_specs=[hbm, hbm, vmem, hbm],
        out_specs=hbm,
        scratch_shapes=[
            pltpu.VMEM((4, 3, UNITS, UNITS), bf16),
            pltpu.VMEM((3, ROWS, UNITS), bf16),
            pltpu.VMEM((ROWS, UNITS), bf16),
            pltpu.VMEM((ITERS, 4, ZC, ROWS, LANES), bf16),
            pltpu.VMEM((NC, 3, ROWS, CW), f32),
            pltpu.VMEM((NC, 3, ROWS, CW), f32),
            pltpu.VMEM((NC, ROWS, CW), f32),
            pltpu.VMEM((NC, ROWS, CW), f32),
            pltpu.VMEM((NC, ROWS, CW), f32),
            pltpu.VMEM((NC, SUB, CW), f32),
            pltpu.VMEM((NC, SUB, CW), f32),
            pltpu.VMEM((NC, 8, CW), f32),
            pltpu.VMEM((2, 1, UNITS), f32),
            pltpu.VMEM((4, 1, UNITS), f32),
            pltpu.VMEM((4, ZC, SUB, LANES), bf16),
            pltpu.VMEM((ITERS, 2, 8, LANES), f32),
            pltpu.VMEM((ITERS, STEPS, 2, 8, LANES), f32),
            pltpu.VMEM((8, LANES), f32),
            pltpu.VMEM((2, ROWS, ROWS), bf16),
            pltpu.VMEM((NC, ROWS, CW), bf16),
            pltpu.VMEM((NC, ROWS, CW), bf16),
            pltpu.VMEM((2, 2, ROWS - SUB, LANES), bf16),
            pltpu.VMEM((2, 2, 2, ROWS - SUB, LANES), bf16),
            pltpu.VMEM((3, 2, SUB, LANES), f32),
            dma((2,)),
            dma((4,)),
            dma((NC,)),
            dma((2,)),
            dma((ITERS, NC)),
            dma((ITERS, NC)),
            dma((ITERS, ZC)),
            dma((ITERS, 3, ZC)),
            dma((3,)),
            dma((3,)),
            dma((ITERS, STEPS)),
            dma((ITERS, STEPS)),
            pltpu.SemaphoreType.REGULAR((4,)),
            dma((2,)),
            dma((2,)),
            dma((2,)),
            dma((2,)),
        ],
        compiler_params=pltpu.CompilerParams(
            collective_id=0, has_side_effects=True, vmem_limit_bytes=58 * 2**20
        ),
    )(jnp.transpose(gate_inputs, (1, 0, 2)), recurrent, initial_state.reshape(8, LANES), guess)


def solution(mesh):
    in_specs = (P("tm", None, "hid"), P(None, None, "hid"), P("hid"), P("tm", "hid"))
    return jax.shard_map(
        per_device, mesh=mesh, in_specs=in_specs, out_specs=P("tm", "hid"), check_vma=False
    )
```

```python
import jax
import jax.numpy as jnp
from jax import lax
from jax.experimental import pallas as pl
from jax.experimental.pallas import tpu as pltpu
from jax.sharding import PartitionSpec as P

ITERS = 2
ROWS = 256
UNITS = 1024
SUB = 16
CW = 256
NC = UNITS // CW
GROUP = 8
LINES = 4
LANES = 128
ZC = UNITS // LANES
XS = 4
STEPS = GROUP * LINES
AWAY = sorted(
    [(a, b, c) for a in range(LINES) for b in range(XS) for c in range(2) if (a, b, c) != (0, 0, 0)],
    key=lambda k: -(min(k[0], LINES - k[0]) + min(k[1], XS - k[1])),
)
MESH = pl.DeviceIdType.MESH


def dot(a, b):
    return jnp.dot(a, b, preferred_element_type=jnp.float32)


def sigmoid(x):
    return 0.5 * jnp.tanh(0.5 * x) + 0.5


def kernel(
    gi, w, h0, guess, out,
    wv, giv, gv, xb, acc, ip, hprev, gs, ss, eg, es, diag, last, edge, top, total, totals, mine, perm, states, terms_own, terms_got, enters,
    load_sem, w_sem, last_sem, right_s, left_s, fwd_s, z_r, edge_s, edge_r, t_s, t_r, known, terms_s, terms_r, enters_s, enters_r,
):
    tm = lax.axis_index("tm")
    z = lax.axis_index("hid")
    y, q = tm // GROUP, lax.rem(tm, GROUP)
    right, left = lax.rem(z + 1, 4), lax.rem(z + 3, 4)

    load_guess = pltpu.make_async_copy(guess, gv, load_sem.at[0])
    load_inputs = pltpu.make_async_copy(gi, giv, load_sem.at[1])

    def load_weights(d):
        rows = pl.ds(pl.multiple_of(lax.rem(z + d, 4) * UNITS, UNITS), UNITS)
        return pltpu.make_async_copy(w.at[:, rows, :], wv.at[d], w_sem.at[d])

    load_guess.start()
    load_weights(0).start()
    load_inputs.start()
    load_weights(1).start()
    load_weights(3).start()

    barrier = pltpu.get_barrier_semaphore()

    def greet(device):
        pl.semaphore_signal(barrier, inc=1, device_id=device, device_id_type=MESH)

    x, core = q // 2, lax.rem(q, 2)

    def device_at(a, b, c):
        return lax.rem(y + a, LINES) * GROUP + lax.rem(x + b, XS) * 2 + lax.rem(core + c, 2)

    x_pair = ((device_at(0, 1, 0), z), (device_at(0, XS - 1, 0), z))
    y_pair = ((device_at(1, 0, 0), z), (device_at(LINES - 1, 0, 0), z))
    partner = ((device_at(0, 0, 1), z),)
    later = (lax.rem(tm + 1, STEPS), z)
    earlier = (lax.rem(tm + STEPS - 1, STEPS), z)
    near = ((tm, right), (tm, left), later, earlier) + x_pair + y_pair + partner
    for device in near:
        greet(device)

    r = lax.broadcasted_iota(jnp.int32, (ROWS, ROWS), 0)
    t = lax.broadcasted_iota(jnp.int32, (ROWS, ROWS), 1)
    time = (r & (SUB - 1)) * SUB + (r >> 4)
    perm[0] = jnp.where(t == time, 1.0, 0.0).astype(jnp.bfloat16)
    perm[1] = jnp.where(t == time - 1, 1.0, 0.0).astype(jnp.bfloat16)

    load_guess.wait()

    last[0] = gv[ROWS - SUB :, :].astype(jnp.float32)[SUB - 1 :, :]
    for n in range(NC):
        rows = dot(perm[1], gv[:, n * CW : (n + 1) * CW])
        hprev[n] = rows
        for k in range(2):
            xb[0, 0, 2 * n + k] = rows[:, k * LANES : (k + 1) * LANES].astype(jnp.bfloat16)

    pl.semaphore_wait(barrier, len(near))

    def remote(src, dst, send, recv, device):
        return pltpu.make_async_remote_copy(
            src_ref=src, dst_ref=dst, send_sem=send, recv_sem=recv, device_id=device, device_id_type=MESH
        )

    half = NC // 2

    def part(it, d, m):
        return xb.at[it, d, pl.ds(2 * m, 2)]

    def to_right(it, m):
        return remote(part(it, 0, m), part(it, 3, m), right_s.at[it, m], z_r.at[it, 0, m], (tm, right))

    def to_left(it, m):
        return remote(part(it, 0, m), part(it, 1, m), left_s.at[it, m], z_r.at[it, 1, m], (tm, left))

    def forward(it, c, size):
        src, device = (3, right) if c < ZC // 2 else (1, left)
        here, there = xb.at[it, src, pl.ds(c, size)], xb.at[it, 2, pl.ds(c, size)]
        return remote(here, there, fwd_s.at[it, c], z_r.at[it, 2, c], (tm, device))

    boundary = remote(last.at[0], last.at[1], last_sem.at[0], last_sem.at[1], later)
    edges = (
        remote(edge.at[0], edge.at[3], edge_s.at[0], edge_r.at[0], (tm, right)),
        remote(edge.at[0], edge.at[1], edge_s.at[1], edge_r.at[1], (tm, left)),
        remote(edge.at[3], edge.at[2], edge_s.at[2], edge_r.at[2], (tm, right)),
    )

    sides = ((tm, right), (tm, left))
    terms_out = [
        remote(terms_own, terms_got.at[k], terms_s.at[k], terms_r.at[k], sides[k]) for k in range(2)
    ]
    enters_out = [
        remote(enters.at[2], enters.at[k], enters_s.at[k], enters_r.at[k], sides[k]) for k in range(2)
    ]

    boundary.start()
    for m in range(half):
        to_right(0, m).start()
        to_left(0, half + m).start()

    def tell(k, devices):
        for device in devices:
            pl.semaphore_signal(known.at[k], inc=1, device_id=device, device_id_type=MESH)

    def hear(k, devices):
        pl.semaphore_wait(known.at[k], len(devices))

    tell(0, x_pair)
    boundary.wait_recv()
    first = lax.broadcasted_iota(jnp.int32, (SUB, LANES), 0) == 0
    for c in range(ZC):
        cols = slice(c * LANES, (c + 1) * LANES)
        edge[0, :, cols] = jnp.where(tm == 0, h0[c : c + 1, :], last[1, :, cols])
    edges[0].start()
    edges[1].start()
    for m in range(half):
        to_right(0, half + m).start()
        to_left(0, m).start()
    for n in range(NC):
        for k in range(2):
            lanes = slice(k * LANES, (k + 1) * LANES)
            row = edge[0, :, n * CW + k * LANES : n * CW + (k + 1) * LANES]
            hprev[n, 0:SUB, lanes] = jnp.where(first, row, hprev[n, 0:SUB, lanes])

    def set_edge(d, pieces):
        for c in pieces:
            row = edge[d, :, c * LANES : (c + 1) * LANES]
            tile = xb[0, d, c, 0:SUB, :].astype(jnp.float32)
            top[d, c] = jnp.where(first, row, tile).astype(jnp.bfloat16)

    hear(0, x_pair)
    tell(1, partner)

    load_inputs.wait()

    for n in range(NC):
        for g in range(3):
            ip[n, g] = dot(perm[0], giv[g, :, n * CW : (n + 1) * CW])

    def block_piece(it, d, c):
        if it > 0:
            return xb[it, d, c]
        return jnp.concatenate([top[d, c], xb[it, d, c, SUB:, :]], axis=0)

    def accumulate(it, pieces, start=False, parts=range(NC)):
        for n in parts:
            cols = slice(n * CW, (n + 1) * CW)
            for g in range(3):
                terms = None if start else acc[n, g]
                for pair in zip(pieces[0::2], pieces[1::2]):
                    rows = jnp.concatenate([block_piece(it, d, c) for d, c in pair], axis=1)
                    (d0, c0), (d1, c1) = pair
                    if (d0, c0 + 1) == (d1, c1):
                        weights = wv[d0, g, c0 * LANES : (c0 + 2) * LANES, cols]
                    else:
                        weights = jnp.concatenate(
                            [wv[d, g, c * LANES : (c + 1) * LANES, cols] for d, c in pair], axis=0
                        )
                    term = dot(rows, weights)
                    terms = term if terms is None else terms + term
                acc[n, g] = terms

    sub_row = lax.broadcasted_iota(jnp.int32, (SUB, CW), 0)

    def tile_of(i):
        return slice(i * SUB, (i + 1) * SUB)

    def total_to(it, away):
        device = device_at(*away)
        copy = remote(total.at[it], totals.at[it, tm], t_s.at[it, device], t_r.at[it, tm], (device, z))
        return device, copy

    def total_from(it, p):
        return remote(total.at[it], totals.at[it, p], t_s.at[it, p], t_r.at[it, p], (tm, right))

    def gates(it, n):
        d0, d1, d2 = (jnp.broadcast_to(diag[n, g : g + 1, :], (SUB, CW)) for g in range(3))
        gain = shift_ = None
        for i in range(ROWS // SUB):
            rows = tile_of(i)
            previous = hprev[n, rows, :]
            memory = acc[n, 2, rows, :]
            update = sigmoid(ip[n, 0, rows, :] + acc[n, 0, rows, :])
            reset = sigmoid(ip[n, 1, rows, :] + acc[n, 1, rows, :])
            candidate = jnp.tanh(ip[n, 2, rows, :] + reset * memory)
            keep = 1.0 - update
            gap = previous - candidate
            target = candidate + update * gap
            slope = update + keep * (
                update * gap * d0
                + (1.0 - candidate * candidate) * reset * ((1.0 - reset) * memory * d1 + d2)
            )
            offset = target - slope * previous
            gain = slope if gain is None else slope * gain
            shift_ = offset if shift_ is None else slope * shift_ + offset
            gs[n, rows, :] = gain
            ss[n, rows, :] = shift_
            if it == 0 and n == 0 and i < ROWS // SUB - 1:
                for k in range(2):
                    lanes = slice(k * LANES, (k + 1) * LANES)
                    terms_own[0, k, rows, :] = gain[:, lanes].astype(jnp.bfloat16)
                    terms_own[1, k, rows, :] = shift_[:, lanes].astype(jnp.bfloat16)
        for k in (1, 2, 4, 8):
            before_gain = jnp.where(sub_row < k, 1.0, pltpu.roll(gain, k, 0))
            before_shift = jnp.where(sub_row < k, 0.0, pltpu.roll(shift_, k, 0))
            shift_ = gain * before_shift + shift_
            gain = gain * before_gain
        eg[n] = jnp.where(sub_row < 1, 1.0, pltpu.roll(gain, 1, 0))
        es[n] = jnp.where(sub_row < 1, 0.0, pltpu.roll(shift_, 1, 0))
        for k in range(2):
            lanes = slice(k * LANES, (k + 1) * LANES)
            row = slice(2 * n + k, 2 * n + k + 1)
            total[it, 0, row, :] = gain[SUB - 1 :, lanes]
            total[it, 1, row, :] = shift_[SUB - 1 :, lanes]

    def send_totals(it):
        for away in AWAY:
            device, copy = total_to(it, away)

            @pl.when(device > tm)
            def _():
                copy.start()

    def enter_block(it):
        def join(p, state):
            total_from(it, p).wait_recv()
            return totals[it, p, 0] * state + totals[it, p, 1]

        mine[...] = lax.fori_loop(0, tm, join, h0[...])

    def enter_of(n):
        row = jnp.concatenate([mine[2 * n : 2 * n + 1, :], mine[2 * n + 1 : 2 * n + 2, :]], axis=1)
        return eg[n] * row + es[n]

    def apply_middle(n):
        enter = enter_of(n)
        hprev[n, 0:SUB, :] = enter
        for k in range(2):
            lanes = slice(k * LANES, (k + 1) * LANES)
            xb[1, 0, 2 * n + k, 0:SUB, :] = enter[:, lanes].astype(jnp.bfloat16)
        for i in range(ROWS // SUB - 1):
            state = gs[n, tile_of(i), :] * enter + ss[n, tile_of(i), :]
            hprev[n, tile_of(i + 1), :] = state
            for k in range(2):
                lanes = slice(k * LANES, (k + 1) * LANES)
                xb[1, 0, 2 * n + k, tile_of(i + 1), :] = state[:, lanes].astype(jnp.bfloat16)
        if n == 0:
            for k in range(2):
                enters[2, k] = enter[:, k * LANES : (k + 1) * LANES]
            for copy in enters_out:
                copy.start()
        else:
            to_right(1, n).start()
            to_left(1, n).start()

    def join_terms(k, d):
        terms_out[k].wait_recv()
        enters_out[k].wait_recv()
        for j in range(2):
            enter = enters[k, j]
            xb[1, d, j, 0:SUB, :] = enter.astype(jnp.bfloat16)
            for i in range(ROWS // SUB - 1):
                gain = terms_got[k, 0, j, tile_of(i), :].astype(jnp.float32)
                shift_ = terms_got[k, 1, j, tile_of(i), :].astype(jnp.float32)
                xb[1, d, j, tile_of(i + 1), :] = (gain * enter + shift_).astype(jnp.bfloat16)

    def apply_last(n):
        enter = enter_of(n)
        for i in range(ROWS // SUB):
            state = gs[n, tile_of(i), :] * enter + ss[n, tile_of(i), :]
            states[n, tile_of(i), :] = state.astype(jnp.bfloat16)
        out[:, n * CW : (n + 1) * CW] = dot(perm[0], states[n]).astype(jnp.bfloat16)

    for it in range(ITERS):
        if it == 0:
            load_weights(0).wait()
            same = r == t
            for n in range(NC):
                block = slice(n * CW, (n + 1) * CW)
                for g in range(3):
                    square = wv[0, g, block, block].astype(jnp.float32)
                    diag[n, g : g + 1, :] = jnp.sum(jnp.where(same, square, 0.0), axis=0, keepdims=True)
            set_edge(0, range(ZC))
        accumulate(it, [(0, c) for c in range(ZC)], True)
        if it == 1:
            join_terms(0, 3)
            forward(it, 0, 2).start()
            join_terms(1, 1)
            accumulate(it, [(3, 0), (3, 1), (1, 0), (1, 1)])
            for m in range(1, NC):
                to_right(it, m).wait_recv()
                to_left(it, m).wait_recv()
                if m == 1:
                    forward(it, 2, 1).start()
                    forward(it, 3, 1).start()
                elif m == 2:
                    forward(it, 4, 2).start()
                else:
                    forward(it, 6, 1).start()
                    forward(it, 7, 1).start()
                accumulate(it, [(d, 2 * m + k) for d in (3, 1) for k in range(2)])
        for m in range(NC if it == 0 else 0):
            opposite = (m + half) % NC
            to_right(it, m).wait_recv()
            to_left(it, opposite).wait_recv()
            if m == 0:
                forward(it, 0, 2).start()
                forward(it, 4, 2).start()
                if it == 0:
                    load_weights(2).start()
                continue
            fresh = [(3, 2 * m), (3, 2 * m + 1), (1, 2 * opposite), (1, 2 * opposite + 1)]
            if m == 1:
                if it == 0:
                    edges[0].wait_recv()
                    edges[2].start()
                for c in (2, 6, 3, 7):
                    forward(it, c, 1).start()
                fresh = [(3, 0), (3, 1), (1, 4), (1, 5)] + fresh
                if it == 0:
                    edges[1].wait_recv()
                    hear(1, partner)
                    tell(2, y_pair)
                    load_weights(1).wait()
                    load_weights(3).wait()
            if it == 0:
                for d, c in fresh:
                    set_edge(d, [c])
            accumulate(it, fresh)
            if it == 0 and m == half:
                hear(2, y_pair)
                tell(3, y_pair)
        if it == 0:
            load_weights(2).wait()
            edges[2].wait_recv()
            hear(3, y_pair)
        for c, size in ((0, 2), (2, 1), (3, 1)):
            forward(it, c, size).wait_recv()
            forward(it, c + ZC // 2, size).wait_recv()
            fresh = [(2, c + k) for k in range(size)] + [(2, c + ZC // 2 + k) for k in range(size)]
            if it == 0:
                for d, k in fresh:
                    set_edge(d, [k])
            if c < 3:
                accumulate(it, fresh)
        for n in range(NC):
            accumulate(it, fresh, parts=[n])
            if n > 0:
                gates(it, n - 1)
            if it == 0 and n == 1:
                for copy in terms_out:
                    copy.start()
        gates(it, NC - 1)
        send_totals(it)
        enter_block(it)
        for n in range(NC):
            (apply_middle if it == 0 else apply_last)(n)

    boundary.wait_send()
    for copy in terms_out + enters_out:
        copy.wait_send()
    for copy in edges:
        copy.wait_send()
    for it in range(ITERS):
        for m in range(it, NC):
            to_right(it, m).wait_send()
            to_left(it, m).wait_send()
        for c, size in ((0, 2), (2, 1), (3, 1)):
            forward(it, c, size).wait_send()
            forward(it, c + ZC // 2, size).wait_send()
        for away in AWAY:
            device, copy = total_to(it, away)

            @pl.when(device > tm)
            def _():
                copy.wait_send()


def per_device(gate_inputs, recurrent, initial_state, guess):
    bf16, f32 = jnp.bfloat16, jnp.float32
    dma = pltpu.SemaphoreType.DMA
    hbm = pl.BlockSpec(memory_space=pl.ANY)
    vmem = pl.BlockSpec(memory_space=pltpu.VMEM)
    return pl.pallas_call(
        kernel,
        out_shape=jax.ShapeDtypeStruct((ROWS, UNITS), bf16),
        in_specs=[hbm, hbm, vmem, hbm],
        out_specs=vmem,
        scratch_shapes=[
            pltpu.VMEM((4, 3, UNITS, UNITS), bf16),
            pltpu.VMEM((3, ROWS, UNITS), bf16),
            pltpu.VMEM((ROWS, UNITS), bf16),
            pltpu.VMEM((ITERS, 4, ZC, ROWS, LANES), bf16),
            pltpu.VMEM((NC, 3, ROWS, CW), f32),
            pltpu.VMEM((NC, 3, ROWS, CW), f32),
            pltpu.VMEM((NC, ROWS, CW), f32),
            pltpu.VMEM((NC, ROWS, CW), f32),
            pltpu.VMEM((NC, ROWS, CW), f32),
            pltpu.VMEM((NC, SUB, CW), f32),
            pltpu.VMEM((NC, SUB, CW), f32),
            pltpu.VMEM((NC, 8, CW), f32),
            pltpu.VMEM((2, 1, UNITS), f32),
            pltpu.VMEM((4, 1, UNITS), f32),
            pltpu.VMEM((4, ZC, SUB, LANES), bf16),
            pltpu.VMEM((ITERS, 2, 8, LANES), f32),
            pltpu.VMEM((ITERS, STEPS, 2, 8, LANES), f32),
            pltpu.VMEM((8, LANES), f32),
            pltpu.VMEM((2, ROWS, ROWS), bf16),
            pltpu.VMEM((NC, ROWS, CW), bf16),
            pltpu.VMEM((2, 2, ROWS - SUB, LANES), bf16),
            pltpu.VMEM((2, 2, 2, ROWS - SUB, LANES), bf16),
            pltpu.VMEM((3, 2, SUB, LANES), f32),
            dma((2,)),
            dma((4,)),
            dma((2,)),
            dma((ITERS, NC)),
            dma((ITERS, NC)),
            dma((ITERS, ZC)),
            dma((ITERS, 3, ZC)),
            dma((3,)),
            dma((3,)),
            dma((ITERS, STEPS)),
            dma((ITERS, STEPS)),
            pltpu.SemaphoreType.REGULAR((4,)),
            dma((2,)),
            dma((2,)),
            dma((2,)),
            dma((2,)),
        ],
        compiler_params=pltpu.CompilerParams(
            collective_id=0, has_side_effects=True, vmem_limit_bytes=53 * 2**20
        ),
    )(jnp.transpose(gate_inputs, (1, 0, 2)), recurrent, initial_state.reshape(8, LANES), guess)


def solution(mesh):
    in_specs = (P("tm", None, "hid"), P(None, None, "hid"), P("hid"), P("tm", "hid"))
    return jax.shard_map(
        per_device, mesh=mesh, in_specs=in_specs, out_specs=P("tm", "hid"), check_vma=False
    )
```

```python
import jax
import jax.numpy as jnp
from jax import lax
from jax.experimental import pallas as pl
from jax.experimental.pallas import tpu as pltpu
from jax.sharding import PartitionSpec as P

ITERS = 2
ROWS = 256
UNITS = 1024
SUB = 16
CW = 256
NC = UNITS // CW
GROUP = 8
LINES = 4
LANES = 128
ZC = UNITS // LANES
XS = 4
STEPS = GROUP * LINES
AWAY = sorted(
    [(a, b, c) for a in range(LINES) for b in range(XS) for c in range(2) if (a, b, c) != (0, 0, 0)],
    key=lambda k: -(min(k[0], LINES - k[0]) + min(k[1], XS - k[1])),
)
MESH = pl.DeviceIdType.MESH


def dot(a, b):
    return jnp.dot(a, b, preferred_element_type=jnp.float32)


def sigmoid(x):
    return 0.5 * jnp.tanh(0.5 * x) + 0.5


def kernel(
    gi, w, h0, guess, out,
    wv, giv, gv, xb, acc, ip, hprev, gs, ss, eg, es, diag, last, edge, top, total, totals, mine, perm, states, terms_own, terms_got, enters,
    load_sem, w_sem, last_sem, right_s, left_s, fwd_s, z_r, edge_s, edge_r, t_s, t_r, known, terms_s, terms_r, enters_s, enters_r,
):
    tm = lax.axis_index("tm")
    z = lax.axis_index("hid")
    y, q = tm // GROUP, lax.rem(tm, GROUP)
    right, left = lax.rem(z + 1, 4), lax.rem(z + 3, 4)

    load_guess = pltpu.make_async_copy(guess, gv, load_sem.at[0])
    load_inputs = pltpu.make_async_copy(gi, giv, load_sem.at[1])

    def load_weights(d):
        rows = pl.ds(pl.multiple_of(lax.rem(z + d, 4) * UNITS, UNITS), UNITS)
        return pltpu.make_async_copy(w.at[:, rows, :], wv.at[d], w_sem.at[d])

    load_guess.start()
    load_weights(0).start()
    load_inputs.start()
    load_weights(1).start()
    load_weights(3).start()

    barrier = pltpu.get_barrier_semaphore()

    def greet(device):
        pl.semaphore_signal(barrier, inc=1, device_id=device, device_id_type=MESH)

    x, core = q // 2, lax.rem(q, 2)

    def device_at(a, b, c):
        return lax.rem(y + a, LINES) * GROUP + lax.rem(x + b, XS) * 2 + lax.rem(core + c, 2)

    x_pair = ((device_at(0, 1, 0), z), (device_at(0, XS - 1, 0), z))
    y_pair = ((device_at(1, 0, 0), z), (device_at(LINES - 1, 0, 0), z))
    partner = ((device_at(0, 0, 1), z),)
    later = (lax.rem(tm + 1, STEPS), z)
    earlier = (lax.rem(tm + STEPS - 1, STEPS), z)
    near = ((tm, right), (tm, left), later, earlier) + x_pair + y_pair + partner
    for device in near:
        greet(device)

    r = lax.broadcasted_iota(jnp.int32, (ROWS, ROWS), 0)
    t = lax.broadcasted_iota(jnp.int32, (ROWS, ROWS), 1)
    time = (r & (SUB - 1)) * SUB + (r >> 4)
    perm[0] = jnp.where(t == time, 1.0, 0.0).astype(jnp.bfloat16)
    perm[1] = jnp.where(t == time - 1, 1.0, 0.0).astype(jnp.bfloat16)

    load_guess.wait()

    last[0] = gv[ROWS - SUB :, :].astype(jnp.float32)[SUB - 1 :, :]
    for n in range(NC):
        rows = dot(perm[1], gv[:, n * CW : (n + 1) * CW])
        hprev[n] = rows
        for k in range(2):
            xb[0, 0, 2 * n + k] = rows[:, k * LANES : (k + 1) * LANES].astype(jnp.bfloat16)

    pl.semaphore_wait(barrier, len(near))

    def remote(src, dst, send, recv, device):
        return pltpu.make_async_remote_copy(
            src_ref=src, dst_ref=dst, send_sem=send, recv_sem=recv, device_id=device, device_id_type=MESH
        )

    half = NC // 2

    def part(it, d, m):
        return xb.at[it, d, pl.ds(2 * m, 2)]

    def to_right(it, m):
        return remote(part(it, 0, m), part(it, 3, m), right_s.at[it, m], z_r.at[it, 0, m], (tm, right))

    def to_left(it, m):
        return remote(part(it, 0, m), part(it, 1, m), left_s.at[it, m], z_r.at[it, 1, m], (tm, left))

    def forward(it, c, size):
        src, device = (3, right) if c < ZC // 2 else (1, left)
        here, there = xb.at[it, src, pl.ds(c, size)], xb.at[it, 2, pl.ds(c, size)]
        return remote(here, there, fwd_s.at[it, c], z_r.at[it, 2, c], (tm, device))

    boundary = remote(last.at[0], last.at[1], last_sem.at[0], last_sem.at[1], later)
    edges = (
        remote(edge.at[0], edge.at[3], edge_s.at[0], edge_r.at[0], (tm, right)),
        remote(edge.at[0], edge.at[1], edge_s.at[1], edge_r.at[1], (tm, left)),
        remote(edge.at[3], edge.at[2], edge_s.at[2], edge_r.at[2], (tm, right)),
    )

    sides = ((tm, right), (tm, left))
    terms_out = [
        remote(terms_own, terms_got.at[k], terms_s.at[k], terms_r.at[k], sides[k]) for k in range(2)
    ]
    enters_out = [
        remote(enters.at[2], enters.at[k], enters_s.at[k], enters_r.at[k], sides[k]) for k in range(2)
    ]

    boundary.start()
    for m in range(half):
        to_right(0, m).start()
        to_left(0, half + m).start()

    def tell(k, devices):
        for device in devices:
            pl.semaphore_signal(known.at[k], inc=1, device_id=device, device_id_type=MESH)

    def hear(k, devices):
        pl.semaphore_wait(known.at[k], len(devices))

    tell(0, x_pair)
    boundary.wait_recv()
    first = lax.broadcasted_iota(jnp.int32, (SUB, LANES), 0) == 0
    for c in range(ZC):
        cols = slice(c * LANES, (c + 1) * LANES)
        edge[0, :, cols] = jnp.where(tm == 0, h0[c : c + 1, :], last[1, :, cols])
    edges[0].start()
    edges[1].start()
    for m in range(half):
        to_right(0, half + m).start()
        to_left(0, m).start()
    for n in range(NC):
        for k in range(2):
            lanes = slice(k * LANES, (k + 1) * LANES)
            row = edge[0, :, n * CW + k * LANES : n * CW + (k + 1) * LANES]
            hprev[n, 0:SUB, lanes] = jnp.where(first, row, hprev[n, 0:SUB, lanes])

    def set_edge(d, pieces):
        for c in pieces:
            row = edge[d, :, c * LANES : (c + 1) * LANES]
            tile = xb[0, d, c, 0:SUB, :].astype(jnp.float32)
            top[d, c] = jnp.where(first, row, tile).astype(jnp.bfloat16)

    hear(0, x_pair)
    tell(1, partner)

    load_inputs.wait()

    for n in range(NC):
        for g in range(3):
            ip[n, g] = dot(perm[0], giv[g, :, n * CW : (n + 1) * CW])

    def block_piece(it, d, c):
        if it > 0:
            return xb[it, d, c]
        return jnp.concatenate([top[d, c], xb[it, d, c, SUB:, :]], axis=0)

    def accumulate(it, pieces, start=False, parts=range(NC)):
        for n in parts:
            cols = slice(n * CW, (n + 1) * CW)
            for g in range(3):
                terms = None if start else acc[n, g]
                for pair in zip(pieces[0::2], pieces[1::2]):
                    rows = jnp.concatenate([block_piece(it, d, c) for d, c in pair], axis=1)
                    (d0, c0), (d1, c1) = pair
                    if (d0, c0 + 1) == (d1, c1):
                        weights = wv[d0, g, c0 * LANES : (c0 + 2) * LANES, cols]
                    else:
                        weights = jnp.concatenate(
                            [wv[d, g, c * LANES : (c + 1) * LANES, cols] for d, c in pair], axis=0
                        )
                    term = dot(rows, weights)
                    terms = term if terms is None else terms + term
                acc[n, g] = terms

    sub_row = lax.broadcasted_iota(jnp.int32, (SUB, CW), 0)

    def tile_of(i):
        return slice(i * SUB, (i + 1) * SUB)

    def total_to(it, away):
        device = device_at(*away)
        copy = remote(total.at[it], totals.at[it, tm], t_s.at[it, device], t_r.at[it, tm], (device, z))
        return device, copy

    def total_from(it, p):
        return remote(total.at[it], totals.at[it, p], t_s.at[it, p], t_r.at[it, p], (tm, right))

    def gates(it, n):
        d0, d1, d2 = (jnp.broadcast_to(diag[n, g : g + 1, :], (SUB, CW)) for g in range(3))
        gain = shift_ = None
        for i in range(ROWS // SUB):
            rows = tile_of(i)
            previous = hprev[n, rows, :]
            memory = acc[n, 2, rows, :]
            update = sigmoid(ip[n, 0, rows, :] + acc[n, 0, rows, :])
            reset = sigmoid(ip[n, 1, rows, :] + acc[n, 1, rows, :])
            candidate = jnp.tanh(ip[n, 2, rows, :] + reset * memory)
            keep = 1.0 - update
            gap = previous - candidate
            target = candidate + update * gap
            slope = update + keep * (
                update * gap * d0
                + (1.0 - candidate * candidate) * reset * ((1.0 - reset) * memory * d1 + d2)
            )
            offset = target - slope * previous
            gain = slope if gain is None else slope * gain
            shift_ = offset if shift_ is None else slope * shift_ + offset
            gs[n, rows, :] = gain
            ss[n, rows, :] = shift_
            if it == 0 and n == 0 and i < ROWS // SUB - 1:
                for k in range(2):
                    lanes = slice(k * LANES, (k + 1) * LANES)
                    terms_own[0, k, rows, :] = gain[:, lanes].astype(jnp.bfloat16)
                    terms_own[1, k, rows, :] = shift_[:, lanes].astype(jnp.bfloat16)
        for k in (1, 2, 4, 8):
            before_gain = jnp.where(sub_row < k, 1.0, pltpu.roll(gain, k, 0))
            before_shift = jnp.where(sub_row < k, 0.0, pltpu.roll(shift_, k, 0))
            shift_ = gain * before_shift + shift_
            gain = gain * before_gain
        eg[n] = jnp.where(sub_row < 1, 1.0, pltpu.roll(gain, 1, 0))
        es[n] = jnp.where(sub_row < 1, 0.0, pltpu.roll(shift_, 1, 0))
        for k in range(2):
            lanes = slice(k * LANES, (k + 1) * LANES)
            row = slice(2 * n + k, 2 * n + k + 1)
            total[it, 0, row, :] = gain[SUB - 1 :, lanes]
            total[it, 1, row, :] = shift_[SUB - 1 :, lanes]

    def send_totals(it):
        for away in AWAY:
            device, copy = total_to(it, away)

            @pl.when(device > tm)
            def _():
                copy.start()

    def enter_block(it):
        def join(p, state):
            total_from(it, p).wait_recv()
            return totals[it, p, 0] * state + totals[it, p, 1]

        mine[...] = lax.fori_loop(0, tm, join, h0[...])

    def enter_of(n):
        row = jnp.concatenate([mine[2 * n : 2 * n + 1, :], mine[2 * n + 1 : 2 * n + 2, :]], axis=1)
        return eg[n] * row + es[n]

    def apply_middle(n):
        enter = enter_of(n)
        hprev[n, 0:SUB, :] = enter
        for k in range(2):
            lanes = slice(k * LANES, (k + 1) * LANES)
            xb[1, 0, 2 * n + k, 0:SUB, :] = enter[:, lanes].astype(jnp.bfloat16)
        for i in range(ROWS // SUB - 1):
            state = gs[n, tile_of(i), :] * enter + ss[n, tile_of(i), :]
            hprev[n, tile_of(i + 1), :] = state
            for k in range(2):
                lanes = slice(k * LANES, (k + 1) * LANES)
                xb[1, 0, 2 * n + k, tile_of(i + 1), :] = state[:, lanes].astype(jnp.bfloat16)
        if n == 0:
            for k in range(2):
                enters[2, k] = enter[:, k * LANES : (k + 1) * LANES]
            for copy in enters_out:
                copy.start()
        else:
            to_right(1, n).start()
            to_left(1, n).start()

    def join_terms(k, d):
        terms_out[k].wait_recv()
        enters_out[k].wait_recv()
        for j in range(2):
            enter = enters[k, j]
            xb[1, d, j, 0:SUB, :] = enter.astype(jnp.bfloat16)
            for i in range(ROWS // SUB - 1):
                gain = terms_got[k, 0, j, tile_of(i), :].astype(jnp.float32)
                shift_ = terms_got[k, 1, j, tile_of(i), :].astype(jnp.float32)
                xb[1, d, j, tile_of(i + 1), :] = (gain * enter + shift_).astype(jnp.bfloat16)

    def apply_last(n):
        enter = enter_of(n)
        for i in range(ROWS // SUB):
            state = gs[n, tile_of(i), :] * enter + ss[n, tile_of(i), :]
            states[n, tile_of(i), :] = state.astype(jnp.bfloat16)
        out[:, n * CW : (n + 1) * CW] = dot(perm[0], states[n]).astype(jnp.bfloat16)

    def drain(it):
        if it == 0:
            boundary.wait_send()
            for copy in edges:
                copy.wait_send()
        else:
            for copy in terms_out + enters_out:
                copy.wait_send()
        for m in range(it, NC):
            to_right(it, m).wait_send()
            to_left(it, m).wait_send()
        for c, size in ((0, 2), (2, 1), (3, 1)):
            forward(it, c, size).wait_send()
            forward(it, c + ZC // 2, size).wait_send()
        for away in AWAY:
            device, copy = total_to(it, away)

            @pl.when(device > tm)
            def _():
                copy.wait_send()

    for it in range(ITERS):
        if it == 0:
            load_weights(0).wait()
            same = r == t
            for n in range(NC):
                block = slice(n * CW, (n + 1) * CW)
                for g in range(3):
                    square = wv[0, g, block, block].astype(jnp.float32)
                    diag[n, g : g + 1, :] = jnp.sum(jnp.where(same, square, 0.0), axis=0, keepdims=True)
            set_edge(0, range(ZC))
        accumulate(it, [(0, c) for c in range(ZC)], True)
        if it == 1:
            join_terms(0, 3)
            forward(it, 0, 2).start()
            join_terms(1, 1)
            drain(0)
            accumulate(it, [(3, 0), (3, 1), (1, 0), (1, 1)])
            for m in range(1, NC):
                to_right(it, m).wait_recv()
                to_left(it, m).wait_recv()
                if m == 1:
                    forward(it, 2, 1).start()
                    forward(it, 3, 1).start()
                elif m == 2:
                    forward(it, 4, 2).start()
                else:
                    forward(it, 6, 1).start()
                    forward(it, 7, 1).start()
                accumulate(it, [(d, 2 * m + k) for d in (3, 1) for k in range(2)])
        for m in range(NC if it == 0 else 0):
            opposite = (m + half) % NC
            to_right(it, m).wait_recv()
            to_left(it, opposite).wait_recv()
            if m == 0:
                forward(it, 0, 2).start()
                forward(it, 4, 2).start()
                if it == 0:
                    load_weights(2).start()
                continue
            fresh = [(3, 2 * m), (3, 2 * m + 1), (1, 2 * opposite), (1, 2 * opposite + 1)]
            if m == 1:
                if it == 0:
                    edges[0].wait_recv()
                    edges[2].start()
                for c in (2, 6, 3, 7):
                    forward(it, c, 1).start()
                fresh = [(3, 0), (3, 1), (1, 4), (1, 5)] + fresh
                if it == 0:
                    edges[1].wait_recv()
                    hear(1, partner)
                    tell(2, y_pair)
                    load_weights(1).wait()
                    load_weights(3).wait()
            if it == 0:
                for d, c in fresh:
                    set_edge(d, [c])
            accumulate(it, fresh)
            if it == 0 and m == half:
                hear(2, y_pair)
                tell(3, y_pair)
        if it == 0:
            load_weights(2).wait()
            edges[2].wait_recv()
            hear(3, y_pair)
        for c, size in ((0, 2), (2, 1), (3, 1)):
            forward(it, c, size).wait_recv()
            forward(it, c + ZC // 2, size).wait_recv()
            fresh = [(2, c + k) for k in range(size)] + [(2, c + ZC // 2 + k) for k in range(size)]
            if it == 0:
                for d, k in fresh:
                    set_edge(d, [k])
            if c < 3:
                accumulate(it, fresh)
        for n in range(NC):
            accumulate(it, fresh, parts=[n])
            if n > 0:
                gates(it, n - 1)
            if it == 0 and n == 1:
                for copy in terms_out:
                    copy.start()
        gates(it, NC - 1)
        send_totals(it)
        enter_block(it)
        for n in range(NC):
            (apply_middle if it == 0 else apply_last)(n)

    drain(1)


def per_device(gate_inputs, recurrent, initial_state, guess):
    bf16, f32 = jnp.bfloat16, jnp.float32
    dma = pltpu.SemaphoreType.DMA
    hbm = pl.BlockSpec(memory_space=pl.ANY)
    vmem = pl.BlockSpec(memory_space=pltpu.VMEM)
    return pl.pallas_call(
        kernel,
        out_shape=jax.ShapeDtypeStruct((ROWS, UNITS), bf16),
        in_specs=[hbm, hbm, vmem, hbm],
        out_specs=vmem,
        scratch_shapes=[
            pltpu.VMEM((4, 3, UNITS, UNITS), bf16),
            pltpu.VMEM((3, ROWS, UNITS), bf16),
            pltpu.VMEM((ROWS, UNITS), bf16),
            pltpu.VMEM((ITERS, 4, ZC, ROWS, LANES), bf16),
            pltpu.VMEM((NC, 3, ROWS, CW), f32),
            pltpu.VMEM((NC, 3, ROWS, CW), f32),
            pltpu.VMEM((NC, ROWS, CW), f32),
            pltpu.VMEM((NC, ROWS, CW), f32),
            pltpu.VMEM((NC, ROWS, CW), f32),
            pltpu.VMEM((NC, SUB, CW), f32),
            pltpu.VMEM((NC, SUB, CW), f32),
            pltpu.VMEM((NC, 8, CW), f32),
            pltpu.VMEM((2, 1, UNITS), f32),
            pltpu.VMEM((4, 1, UNITS), f32),
            pltpu.VMEM((4, ZC, SUB, LANES), bf16),
            pltpu.VMEM((ITERS, 2, 8, LANES), f32),
            pltpu.VMEM((ITERS, STEPS, 2, 8, LANES), f32),
            pltpu.VMEM((8, LANES), f32),
            pltpu.VMEM((2, ROWS, ROWS), bf16),
            pltpu.VMEM((NC, ROWS, CW), bf16),
            pltpu.VMEM((2, 2, ROWS - SUB, LANES), bf16),
            pltpu.VMEM((2, 2, 2, ROWS - SUB, LANES), bf16),
            pltpu.VMEM((3, 2, SUB, LANES), f32),
            dma((2,)),
            dma((4,)),
            dma((2,)),
            dma((ITERS, NC)),
            dma((ITERS, NC)),
            dma((ITERS, ZC)),
            dma((ITERS, 3, ZC)),
            dma((3,)),
            dma((3,)),
            dma((ITERS, STEPS)),
            dma((ITERS, STEPS)),
            pltpu.SemaphoreType.REGULAR((4,)),
            dma((2,)),
            dma((2,)),
            dma((2,)),
            dma((2,)),
        ],
        compiler_params=pltpu.CompilerParams(
            collective_id=0, has_side_effects=True, vmem_limit_bytes=53 * 2**20
        ),
    )(jnp.transpose(gate_inputs, (1, 0, 2)), recurrent, initial_state.reshape(8, LANES), guess)


def solution(mesh):
    in_specs = (P("tm", None, "hid"), P(None, None, "hid"), P("hid"), P("tm", "hid"))
    return jax.shard_map(
        per_device, mesh=mesh, in_specs=in_specs, out_specs=P("tm", "hid"), check_vma=False
    )
```
